32 devices in a mesh: parts: 2 (over x), dp: 16 (over z, y, core).
Axes of the slice: x: 2, y: 2, z: 4, core: 2. Of those that a mesh axis runs over, the one named last changes fastest.
Arguments:
- keys: bfloat16 [128, 512, 512], P(('parts', 'dp')), parts along dimension 0, may hold values from -6 to 6
- values: bfloat16 [128, 512, 512], P(('parts', 'dp')), parts along dimension 0, may hold values from -6 to 6
- lengths: int32 [128], P('parts'), parts along dimension 0, may hold values from 2 to 511
- anchor: int32 [128], P('parts'), parts along dimension 0, may hold values from 0 to 63, as said below
- queries: bfloat16 [128, 4096], P(('parts', 'dp')), parts along dimension 0, may hold values from -128 to 128
- new_keys: bfloat16 [128, 512], P(('parts', 'dp')), parts along dimension 0, may hold values from -6 to 6
- new_values: bfloat16 [128, 512], P(('parts', 'dp')), parts along dimension 0, may hold values from -6 to 6
Outputs:
- cache_keys: bfloat16 [128, 512, 512], P(('parts', 'dp')), parts along dimension 0
- cache_values: bfloat16 [128, 512, 512], P(('parts', 'dp')), parts along dimension 0
- attended: bfloat16 [128, 4096], P(('parts', 'dp')), parts along dimension 0
The draws below stay inside these ranges and needn't reach their ends.
There are 2 independent parts, one for each index of `parts`. The reference program is written for one: setup_inputs(seed, part) draws one part's arguments, and reference() takes and returns one part's arrays. A program takes and returns all parts, laid end to end along the dimension named above; each array names one. Nothing has to cross between parts.
Inputs may be any that keep to these rules, and one draw needn't show every extreme that they name: anchor is a permutation of 0 to 63 with anchor[i] == i wherever anchor[i] is in the group of i; each group's requests that leave go to other groups, at most 2 leave and at most 2 enter each group, every group sends and receives at least one, and some group sends 2.
All inputs are finite; a program needn't handle non-finite values.
Results may differ from the reference program's by a relative error of at most 0.0051.
Values may be sent and summed in bfloat16 or wider, within the bound.
A program may use at most 64 MiB of HBM per device.

```python
import math
import jax
import jax.numpy as jnp
from jax import lax

SLOTS = 4
KVH = 4
QH = 32
HD = 128
GQ = 8
CTX = 512
MOVE = 2
TOTAL = 64


def draw_keys(key, part):
    key = jax.random.fold_in(key, 11)
    sample = jax.random.normal(key, (TOTAL, CTX, KVH * HD), jnp.float32)
    return jnp.clip(sample, -6.0, 6.0).astype(jnp.bfloat16)


def draw_new_keys(key, part):
    key = jax.random.fold_in(key, 13)
    sample = jax.random.normal(key, (TOTAL, KVH * HD), jnp.float32)
    return jnp.clip(sample, -6.0, 6.0).astype(jnp.bfloat16)


def draw_queries(key, part):
    key = jax.random.fold_in(key, 17)
    sample = jax.random.normal(key, (TOTAL, QH * HD), jnp.float32)
    return jnp.clip(sample, -128.0, 128.0).astype(jnp.bfloat16)


def draw_anchor(key, part):
    key = jax.random.fold_in(key, 5)
    group_total = TOTAL // SLOTS
    group_ids = jnp.arange(group_total, dtype=jnp.int32)
    ranking = jax.random.randint(jax.random.fold_in(key, 1), (group_total, SLOTS), 0, 1 << 20)
    ranking = ranking * SLOTS + jnp.arange(SLOTS, dtype=jnp.int32)[None, :]
    slot_order = jnp.argsort(ranking, axis=1).astype(jnp.int32)
    result = jnp.arange(TOTAL, dtype=jnp.int32)
    for round_index in range(MOVE):
        if round_index == 0:
            offset = jax.random.randint(jax.random.fold_in(key, 2), (), 1, group_total)
            sender = (group_ids - offset) % group_total
        else:
            shuffle = jax.random.permutation(jax.random.fold_in(key, 2 + round_index), group_total)
            sender = jnp.argsort(shuffle).astype(jnp.int32)
        dest_slot = group_ids * SLOTS + slot_order[:, round_index]
        source_slot = sender * SLOTS + slot_order[sender, round_index]
        result = result.at[dest_slot].set(source_slot.astype(jnp.int32))
    return result


def set_ends(entries, stream_key, smallest, high):
    extent = entries.shape
    index_at = [jax.random.randint(jax.random.fold_in(stream_key, axis), (), 0, extent[axis]) for axis in range(len(extent))]
    entries = entries.at[tuple(index_at)].set(smallest)
    longest = extent.index(max(extent))
    index_at[longest] = (index_at[longest] + 1) % extent[longest]
    return entries.at[tuple(index_at)].set(high)


def level_of(rng, shape, split, smallest, top_value):
    factor_of, own = 1.0, jax.random.fold_in(rng, 6)
    for position, shards_of in split:
        draws = jnp.exp(jax.random.uniform(jax.random.fold_in(own, position), (shards_of,), jnp.float32, smallest / len(split), top_value / len(split)))
        factor_of = factor_of * jnp.repeat(draws, shape[position] // shards_of).reshape([-1 if axis == position else 1 for axis in range(len(shape))])
    return factor_of


def noise(own_key, dims, deviation, bound, split=(), kind=jnp.bfloat16):
    entries = jax.random.normal(own_key, dims, jnp.float32) * deviation
    if len(split) > 0:
        entries = level_of(own_key, dims, split, -0.22, 0.18) * entries
    return jnp.clip(entries, min=-bound, max=bound).astype(kind)


def setup_inputs(seed: int = 0, part: int = 0) -> dict:
    seeds = jax.random.split(jax.random.key(seed), 8)
    part_keys = jax.random.split(jax.random.fold_in(seeds[7], part), 8)
    return {
        "keys": draw_keys(jax.random.fold_in(jax.random.fold_in(seeds[7], part), 71), part),
        "values": noise(part_keys[1], (TOTAL, CTX, KVH * HD), 1.0, 6.0, ((0, 16),)),
        "lengths": set_ends(jax.random.randint(part_keys[2], (TOTAL,), 2, CTX), jax.random.fold_in(part_keys[2], 1), 2, CTX - 1).astype(jnp.int32),
        "anchor": draw_anchor(jax.random.fold_in(jax.random.fold_in(seeds[7], part), 71), part),
        "queries": draw_queries(jax.random.fold_in(jax.random.fold_in(seeds[7], part), 71), part),
        "new_keys": draw_new_keys(jax.random.fold_in(jax.random.fold_in(seeds[7], part), 71), part),
        "new_values": noise(part_keys[6], (TOTAL, KVH * HD), 1.0, 6.0, ((0, 16),)),
    }


def reference(keys, values, lengths, anchor, queries, new_keys, new_values):
    new_length = lengths[anchor]
    positions = jnp.arange(CTX, dtype=jnp.int32)
    kept = (positions[None, :] < new_length[:, None])[:, :, None]
    written = (positions[None, :] == new_length[:, None])[:, :, None]
    zero_value = jnp.zeros((), keys.dtype)
    cache_keys = jnp.where(written, new_keys[:, None, :], jnp.where(kept, keys[anchor], zero_value))
    cache_values = jnp.where(written, new_values[:, None, :], jnp.where(kept, values[anchor], zero_value))
    query_heads = queries.astype(jnp.float32).reshape(TOTAL, KVH, GQ, HD)
    key_heads = cache_keys.astype(jnp.float32).reshape(TOTAL, CTX, KVH, HD)
    value_heads = cache_values.astype(jnp.float32).reshape(TOTAL, CTX, KVH, HD)
    scores = jnp.einsum('sjgd,scjd->sjgc', query_heads, key_heads) / math.sqrt(HD)
    visible = (positions[None, :] <= new_length[:, None])[:, None, None, :]
    scores = jnp.where(visible, scores, jnp.float32(-1e+30))
    largest = lax.optimization_barrier(jnp.max(scores, axis=-1, keepdims=True))
    powers = jnp.where(visible, jnp.exp(scores - largest), jnp.float32(0.0))
    probs = (powers / lax.optimization_barrier(jnp.sum(powers, axis=-1, keepdims=True))).astype(jnp.bfloat16)
    probs = lax.optimization_barrier(probs)
    result = jnp.einsum('sjgc,scjd->sjgd', probs.astype(jnp.float32), value_heads)
    attended = result.astype(jnp.bfloat16).reshape(TOTAL, QH * HD)
    return (cache_keys, cache_values, attended)
```

```python
import functools
import math

import jax
import jax.numpy as jnp
from jax import lax
from jax.experimental import pallas as pl
from jax.experimental.pallas import tpu as pltpu
from jax.sharding import PartitionSpec as P

HD = 128
ROWS = 16
CHUNKS = 2
MESH = pl.DeviceIdType.MESH
SEND, MOVED, ARRIVAL, LENGTH, FORWARD = 0, 4, 8, 12, 16


def plan_kernel(groups, slots, moves, anchor, lengths, meta, leaving, out_rank):
    me = lax.axis_index("dp")
    total = groups * slots

    def clear(i, c):
        leaving[i] = 0
        return c

    def mark(i, c):
        source = anchor[i]
        leaving[source] = (source // slots != i // slots).astype(jnp.int32)
        return c

    def rank(group, c):
        count = jnp.int32(0)
        for k in range(slots):
            out_rank[group * slots + k] = count
            count = count + leaving[group * slots + k]
        return c

    def forward(group, c):
        for e in range(moves):
            meta[FORWARD + group * moves + e] = 0
        count = jnp.int32(0)
        for k in range(slots):
            source = anchor[group * slots + k]
            moved = source // slots != group

            @pl.when(moved)
            def _():
                meta[FORWARD + group * moves + count] = source // slots * moves + out_rank[source]

            @pl.when(group == me)
            def _():
                meta[MOVED + k] = moved.astype(jnp.int32)
                meta[ARRIVAL + k] = jnp.where(moved, count, 0)
                meta[LENGTH + k] = lengths[source]

            count = count + moved.astype(jnp.int32)
        return c

    lax.fori_loop(0, total, clear, 0)
    lax.fori_loop(0, total, mark, 0)
    lax.fori_loop(0, groups, rank, 0)
    lax.fori_loop(0, groups, forward, 0)
    for e in range(slots):
        meta[SEND + e] = 0
    for k in range(slots):
        @pl.when(leaving[me * slots + k] == 1)
        def _():
            meta[SEND + out_rank[me * slots + k]] = k


def migrate_kernel(groups, slots, moves, chunks, meta, keys, values, out, *scratch):
    kv, send1, send2 = scratch[:3]
    recv1 = scratch[3 : 3 + chunks]
    load_sem, s1_sem, r1_sem, s2_sem, r2_sem, own_sem = scratch[3 + chunks :]
    me = lax.axis_index("dp")
    half = groups // 2
    depth = send1.shape[3]
    piece = depth * chunks

    loads = [
        pltpu.make_async_copy(keys, kv.at[pl.ds(0, slots)], load_sem.at[0]),
        pltpu.make_async_copy(values, kv.at[pl.ds(slots, slots)], load_sem.at[1]),
    ]
    for load in loads:
        load.start()
    barrier = pltpu.get_barrier_semaphore()

    def greet(d, c):
        pl.semaphore_signal(
            barrier, inc=1, device_id={"dp": lax.rem(me + d, groups)}, device_id_type=MESH
        )
        return c

    lax.fori_loop(1, groups, greet, 0)
    for load in loads:
        load.wait()
    pl.semaphore_wait(barrier, groups - 1)

    def hop1(chunk, peer, sender):
        return pltpu.make_async_remote_copy(
            src_ref=send1.at[chunk, peer],
            dst_ref=recv1[chunk].at[pl.ds(sender * moves, moves)],
            send_sem=s1_sem.at[chunk, peer],
            recv_sem=r1_sem.at[chunk, sender],
            device_id={"dp": peer},
            device_id_type=MESH,
        )

    def hop2(chunk, peer, sender):
        return pltpu.make_async_remote_copy(
            src_ref=send2.at[chunk, peer],
            dst_ref=out.at[sender, :, pl.ds(chunk * depth, depth)],
            send_sem=s2_sem.at[chunk, peer],
            recv_sem=r2_sem.at[chunk, sender],
            device_id={"dp": peer},
            device_id_type=MESH,
        )

    def own_copy(chunk):
        return pltpu.make_async_copy(
            send2.at[chunk, me], out.at[me, :, pl.ds(chunk * depth, depth)], own_sem.at[chunk]
        )

    def pack(chunk, peer, e):
        row = pl.multiple_of(lax.rem(peer, half) * piece + chunk * depth, ROWS)
        return kv[peer // half * slots + meta[SEND + e], pl.ds(row, depth)]

    for chunk in range(chunks):

        def start1(d, c):
            peer = lax.rem(me + d, groups)
            for e in range(moves):
                send1[chunk, peer, e] = pack(chunk, peer, e)
            hop1(chunk, peer, me).start()
            return c

        lax.fori_loop(1, groups, start1, 0)
        for e in range(moves):
            recv1[chunk][me * moves + e] = pack(chunk, me, e)

    for chunk in range(chunks):

        def wait1(d, c):
            sender = lax.rem(me + groups - d, groups)
            hop1(chunk, sender, sender).wait_recv()
            return c

        def fill(peer):
            for e in range(moves):
                send2[chunk, peer, e] = recv1[chunk][meta[FORWARD + peer * moves + e]]

        def start2(d, c):
            peer = lax.rem(me + d, groups)
            fill(peer)
            hop2(chunk, peer, me).start()
            return c

        lax.fori_loop(1, groups, wait1, 0)
        lax.fori_loop(1, groups, start2, 0)
        fill(me)
        own_copy(chunk).start()

    for chunk in range(chunks):

        def finish(d, c):
            peer = lax.rem(me + d, groups)
            sender = lax.rem(me + groups - d, groups)
            hop1(chunk, peer, me).wait_send()
            hop2(chunk, sender, sender).wait_recv()
            hop2(chunk, peer, me).wait_send()
            return c

        lax.fori_loop(1, groups, finish, 0)
        own_copy(chunk).wait()


def attend_kernel(meta, keys, values, arrived, queries, new_keys, new_values, out_k, out_v, out_a):
    slot = pl.program_id(0)
    moved = meta[MOVED + slot] == 1
    length = meta[LENGTH + slot]
    context, width = keys.shape[1:]
    per_group = queries.shape[1] // (width // HD)
    position = lax.broadcasted_iota(jnp.int32, (context, width), 0)

    def build(kind, own, token, out):
        @pl.when(moved)
        def _():
            out[0] = arrived[kind, :, 0].reshape(context, width)

        @pl.when(jnp.logical_not(moved))
        def _():
            out[0] = own[0]

        row = jnp.where(position == length, token[0], jnp.zeros((), out.dtype))
        out[0] = jnp.where(position < length, out[0], row)

    build(0, keys, new_keys, out_k)
    build(1, values, new_values, out_v)
    visible = lax.broadcasted_iota(jnp.int32, (per_group, context), 1) <= length
    for head in range(width // HD):
        lanes = slice(head * HD, (head + 1) * HD)
        rows = slice(head * per_group, (head + 1) * per_group)
        scores = lax.dot_general(
            queries[0, rows],
            out_k[0, :, lanes],
            (((1,), (1,)), ((), ())),
            preferred_element_type=jnp.float32,
        ) / math.sqrt(HD)
        scores = jnp.where(visible, scores, jnp.float32(-1e30))
        powers = jnp.exp(scores - jnp.max(scores, axis=-1, keepdims=True))
        powers = jnp.where(visible, powers, jnp.float32(0.0))
        probs = (powers / jnp.sum(powers, axis=-1, keepdims=True)).astype(jnp.bfloat16)
        result = jnp.dot(probs, out_v[0, :, lanes], preferred_element_type=jnp.float32)
        out_a[0, rows] = result.astype(out_a.dtype)


def local(keys, values, lengths, anchor, queries, new_keys, new_values):
    groups = lax.axis_size("dp")
    slots, context, width = keys.shape
    moves = (slots + 1) // 2
    half = groups // 2
    piece = context // half
    chunks = max(1, min(CHUNKS, piece // ROWS))
    depth = piece // chunks
    total = groups * slots
    kind = keys.dtype
    params = functools.partial(pltpu.CompilerParams, vmem_limit_bytes=40 << 20)
    smem = pl.BlockSpec(memory_space=pltpu.SMEM)
    hbm = pl.BlockSpec(memory_space=pl.ANY)

    meta = pl.pallas_call(
        functools.partial(plan_kernel, groups, slots, moves),
        out_shape=jax.ShapeDtypeStruct((FORWARD + groups * moves,), jnp.int32),
        in_specs=[smem, smem],
        out_specs=smem,
        scratch_shapes=[pltpu.SMEM((total,), jnp.int32), pltpu.SMEM((total,), jnp.int32)],
    )(anchor, lengths)

    dma = pltpu.SemaphoreType.DMA
    arrived = pl.pallas_call(
        functools.partial(migrate_kernel, groups, slots, moves, chunks),
        out_shape=jax.ShapeDtypeStruct((groups, moves, piece, width), kind),
        in_specs=[smem, hbm, hbm],
        out_specs=hbm,
        scratch_shapes=[
            pltpu.VMEM((2 * slots, context, width), kind),
            pltpu.VMEM((chunks, groups, moves, depth, width), kind),
            pltpu.VMEM((chunks, groups, moves, depth, width), kind),
        ]
        + [pltpu.VMEM((groups * moves, depth, width), kind) for _ in range(chunks)]
        + [dma((2,))]
        + [dma((chunks, groups)) for _ in range(4)]
        + [dma((chunks,))],
        compiler_params=params(collective_id=0, has_side_effects=True),
    )(meta, keys, values)
    arrived = arrived.reshape(2, half, moves, piece, width)

    heads = queries.shape[1] // HD
    cache = pl.BlockSpec((1, context, width), lambda i, m: (i, 0, 0))
    token = pl.BlockSpec((1, 1, width), lambda i, m: (i, 0, 0))
    query = pl.BlockSpec((1, heads, HD), lambda i, m: (i, 0, 0))
    landed = pl.BlockSpec(
        (2, half, 1, piece, width), lambda i, m: (0, 0, m[ARRIVAL + i], 0, 0)
    )
    cache_keys, cache_values, attended = pl.pallas_call(
        attend_kernel,
        out_shape=(
            jax.ShapeDtypeStruct(keys.shape, kind),
            jax.ShapeDtypeStruct(values.shape, kind),
            jax.ShapeDtypeStruct((slots, heads, HD), queries.dtype),
        ),
        grid_spec=pltpu.PrefetchScalarGridSpec(
            num_scalar_prefetch=1,
            grid=(slots,),
            in_specs=[cache, cache, landed, query, token, token],
            out_specs=(cache, cache, query),
        ),
        compiler_params=params(),
    )(
        meta,
        keys,
        values,
        arrived,
        queries.reshape(slots, heads, HD),
        new_keys[:, None],
        new_values[:, None],
    )
    return (cache_keys, cache_values, attended.reshape(queries.shape))


def solution(mesh):
    in_specs = (
        P(("parts", "dp"), None, None),
        P(("parts", "dp"), None, None),
        P("parts"),
        P("parts"),
        P(("parts", "dp"), None),
        P(("parts", "dp"), None),
        P(("parts", "dp"), None),
    )
    out_specs = (
        P(("parts", "dp"), None, None),
        P(("parts", "dp"), None, None),
        P(("parts", "dp"), None),
    )
    return jax.shard_map(local, mesh=mesh, in_specs=in_specs, out_specs=out_specs, check_vma=False)
```

```python
import functools
import math

import jax
import jax.numpy as jnp
from jax import lax
from jax.experimental import pallas as pl
from jax.experimental.pallas import tpu as pltpu
from jax.sharding import PartitionSpec as P

HD = 128
ROWS = 16
CHUNKS = 2
MESH = pl.DeviceIdType.MESH


def moved_at(anchor, index):
    return (anchor[index] != index).astype(jnp.int32)


def rank_of(anchor, slot, slots):
    first = slot // slots * slots
    count = jnp.int32(0)
    for k in range(slots - 1):
        count = count + moved_at(anchor, first + k) * (first + k < slot).astype(jnp.int32)
    return count


def moved_slot(anchor, group, slots, e):
    found, count = jnp.int32(0), jnp.int32(0)
    for k in range(slots):
        moved = moved_at(anchor, group * slots + k)
        found = found + k * moved * (count == e).astype(jnp.int32)
        count = count + moved
    return found


def row_of(tokens, slot):
    rows = lax.broadcasted_iota(jnp.int32, tokens.shape, 0)
    picked = jnp.where(rows == slot, tokens[...].astype(jnp.float32), 0.0)
    return jnp.sum(picked, axis=0, keepdims=True).astype(tokens.dtype)


def placed(rows, token, length):
    position = lax.broadcasted_iota(jnp.int32, rows.shape, 0)
    tail = jnp.where(position == length, token, jnp.zeros((), rows.dtype))
    return jnp.where(position < length, rows, tail)


def attend(queries, keys, values, length):
    scores = lax.dot_general(
        queries, keys, (((1,), (1,)), ((), ())), preferred_element_type=jnp.float32
    ) / math.sqrt(HD)
    visible = lax.broadcasted_iota(jnp.int32, scores.shape, 1) <= length
    scores = jnp.where(visible, scores, jnp.float32(-1e30))
    powers = jnp.exp(scores - jnp.max(scores, axis=-1, keepdims=True))
    powers = jnp.where(visible, powers, jnp.float32(0.0))
    probs = (powers / jnp.sum(powers, axis=-1, keepdims=True)).astype(jnp.bfloat16)
    result = jnp.dot(probs, values, preferred_element_type=jnp.float32)
    return result.astype(jnp.bfloat16)


def migrate_kernel(
    groups, slots, moves, chunks, anchor, lengths, keys, values, queries, new_keys, new_values,
    out, kept, *scratch
):
    kv, send1, send2 = scratch[:3]
    recv1 = scratch[3 : 3 + chunks]
    load_sem, s1_sem, r1_sem, s2_sem, r2_sem, own_sem = scratch[3 + chunks :]
    me = lax.axis_index("dp")
    half = groups // 2
    depth = send1.shape[3]
    piece = depth * chunks

    loads = [
        pltpu.make_async_copy(keys, kv.at[pl.ds(0, slots)], load_sem.at[0]),
        pltpu.make_async_copy(values, kv.at[pl.ds(slots, slots)], load_sem.at[1]),
    ]
    for load in loads:
        load.start()
    barrier = pltpu.get_barrier_semaphore()

    def greet(d, c):
        pl.semaphore_signal(
            barrier, inc=1, device_id={"dp": lax.rem(me + d, groups)}, device_id_type=MESH
        )
        return c

    lax.fori_loop(1, groups, greet, 0)
    for load in loads:
        load.wait()
    pl.semaphore_wait(barrier, groups - 1)

    leave = [moved_slot(anchor, me, slots, e) for e in range(moves)]

    def hop1(chunk, peer, sender):
        return pltpu.make_async_remote_copy(
            src_ref=send1.at[chunk, peer],
            dst_ref=recv1[chunk].at[pl.ds(sender * moves, moves)],
            send_sem=s1_sem.at[chunk, peer],
            recv_sem=r1_sem.at[chunk, sender],
            device_id={"dp": peer},
            device_id_type=MESH,
        )

    def hop2(chunk, peer, sender):
        return pltpu.make_async_remote_copy(
            src_ref=send2.at[chunk, peer],
            dst_ref=out.at[sender, :, pl.ds(chunk * depth, depth)],
            send_sem=s2_sem.at[chunk, peer],
            recv_sem=r2_sem.at[chunk, sender],
            device_id={"dp": peer},
            device_id_type=MESH,
        )

    def own_copy(chunk):
        return pltpu.make_async_copy(
            send2.at[chunk, me], out.at[me, :, pl.ds(chunk * depth, depth)], own_sem.at[chunk]
        )

    def pack(chunk, peer, e):
        row = pl.multiple_of(lax.rem(peer, half) * piece + chunk * depth, ROWS)
        return kv[peer // half * slots + leave[e], pl.ds(row, depth)]

    for chunk in range(chunks):

        def start1(d, c):
            peer = lax.rem(me + d, groups)
            for e in range(moves):
                send1[chunk, peer, e] = pack(chunk, peer, e)
            hop1(chunk, peer, me).start()
            return c

        lax.fori_loop(1, groups, start1, 0)
        for e in range(moves):
            recv1[chunk][me * moves + e] = pack(chunk, me, e)

    def resident(slot, c):
        length = lengths[me * slots + slot]
        token_k, token_v = row_of(new_keys, slot), row_of(new_values, slot)
        per_group = queries.shape[1] // (kv.shape[2] // HD)
        for head in range(kv.shape[2] // HD):
            lanes = slice(head * HD, (head + 1) * HD)
            rows = slice(head * per_group, (head + 1) * per_group)
            kept[slot, rows] = attend(
                queries[slot, rows],
                placed(kv[slot, :, lanes], token_k[:, lanes], length),
                placed(kv[slots + slot, :, lanes], token_v[:, lanes], length),
                length,
            )
        return c

    lax.fori_loop(0, slots, resident, 0)

    for chunk in range(chunks):

        def wait1(d, c):
            sender = lax.rem(me + groups - d, groups)
            hop1(chunk, sender, sender).wait_recv()
            return c

        def fill(peer):
            for e in range(moves):
                source = anchor[peer * slots + moved_slot(anchor, peer, slots, e)]
                rank = jnp.minimum(rank_of(anchor, source, slots), moves - 1)
                send2[chunk, peer, e] = recv1[chunk][source // slots * moves + rank]

        def start2(d, c):
            peer = lax.rem(me + d, groups)
            fill(peer)
            hop2(chunk, peer, me).start()
            return c

        lax.fori_loop(1, groups, wait1, 0)
        lax.fori_loop(1, groups, start2, 0)
        fill(me)
        own_copy(chunk).start()

    for chunk in range(chunks):

        def finish(d, c):
            peer = lax.rem(me + d, groups)
            sender = lax.rem(me + groups - d, groups)
            hop1(chunk, peer, me).wait_send()
            hop2(chunk, sender, sender).wait_recv()
            hop2(chunk, peer, me).wait_send()
            return c

        lax.fori_loop(1, groups, finish, 0)
        own_copy(chunk).wait()


def arrival_of(anchor, me, slots, moves, slot):
    count = jnp.int32(0)
    for k in range(slots):
        count = count + moved_at(anchor, me * slots + k) * (k <= slot).astype(jnp.int32)
    return jnp.clip(count - 1, 0, moves - 1)


def place_kernel(
    slots, own, anchor, lengths, keys, values, arrived, kept, queries, new_keys, new_values,
    out_k, out_v, out_a
):
    slot = pl.program_id(0)
    index = own[0] * slots + slot
    length = lengths[anchor[index]]
    context, width = keys.shape[1:]
    per_group = queries.shape[1] // (width // HD)
    token_k, token_v = row_of(new_keys, slot), row_of(new_values, slot)

    @pl.when(anchor[index] == index)
    def _():
        out_k[0] = placed(keys[0], token_k, length)
        out_v[0] = placed(values[0], token_v, length)
        out_a[0] = kept[0]

    @pl.when(anchor[index] != index)
    def _():
        out_k[0] = placed(arrived[0, :, 0].reshape(context, width), token_k, length)
        out_v[0] = placed(arrived[1, :, 0].reshape(context, width), token_v, length)
        for head in range(width // HD):
            lanes = slice(head * HD, (head + 1) * HD)
            rows = slice(head * per_group, (head + 1) * per_group)
            out_a[0, rows] = attend(
                queries[0, rows], out_k[0, :, lanes], out_v[0, :, lanes], length
            )


def local(keys, values, lengths, anchor, queries, new_keys, new_values):
    groups = lax.axis_size("dp")
    slots, context, width = keys.shape
    moves = (slots + 1) // 2
    half = groups // 2
    piece = context // half
    chunks = max(1, min(CHUNKS, piece // ROWS))
    depth = piece // chunks
    kind = keys.dtype
    params = functools.partial(pltpu.CompilerParams, vmem_limit_bytes=56 << 20)
    smem = pl.BlockSpec(memory_space=pltpu.SMEM)
    hbm = pl.BlockSpec(memory_space=pl.ANY)

    dma = pltpu.SemaphoreType.DMA
    vmem = pl.BlockSpec(memory_space=pltpu.VMEM)
    heads = queries.shape[1] // HD
    tall = queries.reshape(slots, heads, HD)
    arrived, kept = pl.pallas_call(
        functools.partial(migrate_kernel, groups, slots, moves, chunks),
        out_shape=(
            jax.ShapeDtypeStruct((groups, moves, piece, width), kind),
            jax.ShapeDtypeStruct(tall.shape, tall.dtype),
        ),
        in_specs=[smem, smem, hbm, hbm, vmem, vmem, vmem],
        out_specs=(hbm, vmem),
        scratch_shapes=[
            pltpu.VMEM((2 * slots, context, width), kind),
            pltpu.VMEM((chunks, groups, moves, depth, width), kind),
            pltpu.VMEM((chunks, groups, moves, depth, width), kind),
        ]
        + [pltpu.VMEM((groups * moves, depth, width), kind) for _ in range(chunks)]
        + [dma((2,))]
        + [dma((chunks, groups)) for _ in range(4)]
        + [dma((chunks,))],
        compiler_params=params(collective_id=0, has_side_effects=True),
    )(anchor, lengths, keys, values, tall, new_keys, new_values)
    arrived = arrived.reshape(2, half, moves, piece, width)

    def landed(i, own, anchor, lengths):
        return (0, 0, arrival_of(anchor, own[0], slots, moves, i), 0, 0)

    cache = pl.BlockSpec((1, context, width), lambda i, *_: (i, 0, 0))
    token = pl.BlockSpec((slots, width), lambda i, *_: (0, 0))
    query = pl.BlockSpec((1, heads, HD), lambda i, *_: (i, 0, 0))
    cache_keys, cache_values, attended = pl.pallas_call(
        functools.partial(place_kernel, slots),
        out_shape=(
            jax.ShapeDtypeStruct(keys.shape, kind),
            jax.ShapeDtypeStruct(values.shape, kind),
            jax.ShapeDtypeStruct(tall.shape, tall.dtype),
        ),
        grid_spec=pltpu.PrefetchScalarGridSpec(
            num_scalar_prefetch=3,
            grid=(slots,),
            in_specs=[
                cache,
                cache,
                pl.BlockSpec((2, half, 1, piece, width), landed),
                query,
                query,
                token,
                token,
            ],
            out_specs=(cache, cache, query),
        ),
        compiler_params=params(),
    )(
        lax.axis_index("dp").reshape(1),
        anchor,
        lengths,
        keys,
        values,
        arrived,
        kept,
        tall,
        new_keys,
        new_values,
    )
    return (cache_keys, cache_values, attended.reshape(queries.shape))


def solution(mesh):
    in_specs = (
        P(("parts", "dp"), None, None),
        P(("parts", "dp"), None, None),
        P("parts"),
        P("parts"),
        P(("parts", "dp"), None),
        P(("parts", "dp"), None),
        P(("parts", "dp"), None),
    )
    out_specs = (
        P(("parts", "dp"), None, None),
        P(("parts", "dp"), None, None),
        P(("parts", "dp"), None),
    )
    return jax.shard_map(local, mesh=mesh, in_specs=in_specs, out_specs=out_specs, check_vma=False)
```

```python
import functools
import math

import jax
import jax.numpy as jnp
from jax import lax
from jax.experimental import pallas as pl
from jax.experimental.pallas import tpu as pltpu
from jax.sharding import PartitionSpec as P

HD = 128
ROWS = 16
CHUNKS = 2
SHARES = (0.28, 0.36, 0.44, 0.58, 1.0)
MESH = pl.DeviceIdType.MESH


def moved_at(anchor, index):
    return (anchor[index] != index).astype(jnp.int32)


def rank_of(anchor, slot, slots):
    first = slot // slots * slots
    count = jnp.int32(0)
    for k in range(slots - 1):
        count = count + moved_at(anchor, first + k) * (first + k < slot).astype(jnp.int32)
    return count


def moved_slot(anchor, group, slots, e):
    found, count = jnp.int32(0), jnp.int32(0)
    for k in range(slots):
        moved = moved_at(anchor, group * slots + k)
        found = found + k * moved * (count == e).astype(jnp.int32)
        count = count + moved
    return found


def row_of(tokens, slot):
    rows = lax.broadcasted_iota(jnp.int32, tokens.shape, 0)
    picked = jnp.where(rows == slot, tokens[...].astype(jnp.float32), 0.0)
    return jnp.sum(picked, axis=0, keepdims=True).astype(tokens.dtype)


def placed(rows, token, length):
    position = lax.broadcasted_iota(jnp.int32, rows.shape, 0)
    tail = jnp.where(position == length, token, jnp.zeros((), rows.dtype))
    return jnp.where(position < length, rows, tail)


def attend(queries, keys, values, length):
    scores = lax.dot_general(
        queries, keys, (((1,), (1,)), ((), ())), preferred_element_type=jnp.float32
    ) / math.sqrt(HD)
    visible = lax.broadcasted_iota(jnp.int32, scores.shape, 1) <= length
    scores = jnp.where(visible, scores, jnp.float32(-1e30))
    powers = jnp.exp(scores - jnp.max(scores, axis=-1, keepdims=True))
    powers = jnp.where(visible, powers, jnp.float32(0.0))
    probs = (powers / jnp.sum(powers, axis=-1, keepdims=True)).astype(jnp.bfloat16)
    result = jnp.dot(probs, values, preferred_element_type=jnp.float32)
    return result.astype(jnp.bfloat16)


def plan_kernel(groups, slots, moves, units, unit_rows, anchor, lengths, own, need, offset, table, target):
    side = groups // 2
    mine = own[0] // side

    def invert(i, c):
        target[anchor[i]] = i
        return c

    lax.fori_loop(0, groups * slots, invert, 0, unroll=8)
    most = jnp.int32(0)
    for half in range(2):

        def each(k, count):
            slot = half * side * slots + k
            group = slot // slots
            crosses = target[slot] // slots // side != half
            offset[slot] = count
            rank = jnp.minimum(rank_of(anchor, slot, slots), moves - 1)
            first = ((group - half * side) * moves + rank) * units

            @pl.when(jnp.logical_and(crosses, mine == half))
            def _():
                for t in range(units):
                    table[count + t] = first + t

            taken = (lengths[slot] + unit_rows - 1) // unit_rows
            return count + jnp.where(crosses, taken, 0)

        most = jnp.maximum(most, lax.fori_loop(0, side * slots, each, jnp.int32(0)))
    need[0] = most


def migrate_kernel(
    groups, slots, moves, chunks, size, anchor, lengths, offset, table, keys, values, queries,
    new_keys, new_values, out, kept, *scratch
):
    kv, send1, send2, send3 = scratch[:4]
    recv1 = scratch[4 : 4 + chunks]
    recv2 = scratch[4 + chunks : 4 + 2 * chunks]
    load_sem, s1_sem, r1_sem, s2_sem, r2_sem, s3_sem, r3_sem, own_sem = scratch[4 + 2 * chunks :]
    me = lax.axis_index("dp")
    side = groups // 2
    half, seat = me // side, lax.rem(me, side)
    base = half * side
    partner = (1 - half) * side + seat
    units, parts = kv.shape[1:3]
    width = kv.shape[5]
    heads = width // HD
    context = units * parts * chunks * ROWS

    loads = [
        pltpu.make_async_copy(keys, kv.at[pl.ds(0, slots)], load_sem.at[0]),
        pltpu.make_async_copy(values, kv.at[pl.ds(slots, slots)], load_sem.at[1]),
    ]
    for load in loads:
        load.start()
    barrier = pltpu.get_barrier_semaphore()

    def greet(d, c):
        peer = base + lax.rem(seat + d, side)
        pl.semaphore_signal(barrier, inc=1, device_id={"dp": peer}, device_id_type=MESH)
        return c

    lax.fori_loop(1, side, greet, 0)
    pl.semaphore_signal(barrier, inc=1, device_id={"dp": partner}, device_id_type=MESH)
    for chunk in range(chunks):
        recv2[chunk][pl.ds(size, units)] = jnp.zeros((units, ROWS, HD), kv.dtype)
    leave = [moved_slot(anchor, me, slots, e) for e in range(moves)]
    for load in loads:
        load.wait()
    pl.semaphore_wait(barrier, side)

    def hop1(chunk, peer, sender):
        return pltpu.make_async_remote_copy(
            src_ref=send1.at[chunk, peer],
            dst_ref=recv1[chunk].at[pl.ds(sender * moves * units, moves * units)],
            send_sem=s1_sem.at[chunk, peer],
            recv_sem=r1_sem.at[chunk, sender],
            device_id={"dp": base + peer},
            device_id_type=MESH,
        )

    def hop2(chunk):
        return pltpu.make_async_remote_copy(
            src_ref=send2.at[chunk],
            dst_ref=recv2[chunk].at[pl.ds(0, size)],
            send_sem=s2_sem.at[chunk],
            recv_sem=r2_sem.at[chunk],
            device_id={"dp": partner},
            device_id_type=MESH,
        )

    def hop3(chunk, peer, sender):
        return pltpu.make_async_remote_copy(
            src_ref=send3.at[chunk, peer],
            dst_ref=out.at[sender, chunk],
            send_sem=s3_sem.at[chunk, peer],
            recv_sem=r3_sem.at[chunk, sender],
            device_id={"dp": base + peer},
            device_id_type=MESH,
        )

    def own_copy(chunk):
        return pltpu.make_async_copy(send3.at[chunk, seat], out.at[seat, chunk], own_sem.at[chunk])

    def pack(chunk, peer, e):
        column = peer // parts
        lane = pl.multiple_of(lax.rem(column, heads) * HD, HD)
        return kv[
            column // heads * slots + leave[e], :, lax.rem(peer, parts), chunk, :, pl.ds(lane, HD)
        ]

    for chunk in range(chunks):

        def start1(d, c):
            peer = lax.rem(seat + d, side)
            for e in range(moves):
                send1[chunk, peer, pl.ds(e * units, units)] = pack(chunk, peer, e)
            hop1(chunk, peer, seat).start()
            return c

        lax.fori_loop(1, side, start1, 0)
        for e in range(moves):
            recv1[chunk][pl.ds((seat * moves + e) * units, units)] = pack(chunk, seat, e)

    def resident(slot, c):
        length = lengths[me * slots + slot]
        token_k, token_v = row_of(new_keys, slot), row_of(new_values, slot)
        per_group = queries.shape[1] // heads
        for head in range(heads):
            lanes = slice(head * HD, (head + 1) * HD)
            rows = slice(head * per_group, (head + 1) * per_group)
            key_rows = kv[slot, :, :, :, :, lanes].reshape(context, HD)
            value_rows = kv[slots + slot, :, :, :, :, lanes].reshape(context, HD)
            kept[slot, rows] = attend(
                queries[slot, rows],
                placed(key_rows, token_k[:, lanes], length),
                placed(value_rows, token_v[:, lanes], length),
                length,
            )
        return c

    lax.fori_loop(0, slots, resident, 0)

    def wait1(chunk):
        def step(d, c):
            sender = lax.rem(seat + side - d, side)
            hop1(chunk, sender, sender).wait_recv()
            return c

        lax.fori_loop(1, side, step, 0)

    for chunk in range(chunks):
        wait1(chunk)

        def fill2(u, c):
            for k in range(4):
                place = jnp.clip(table[u * 4 + k], 0, recv1[chunk].shape[0] - 1)
                send2[chunk, u * 4 + k] = recv1[chunk][place]
            return c

        lax.fori_loop(0, size // 4, fill2, 0)
        hop2(chunk).start()

    for chunk in range(chunks):
        hop2(chunk).wait_recv()

        def fill3(peer):
            group = base + peer
            for e in range(moves):
                source = anchor[group * slots + moved_slot(anchor, group, slots, e)]
                rank = jnp.minimum(rank_of(anchor, source, slots), moves - 1)
                holder = source // slots
                near = holder // side == half
                local = jnp.where(near, ((holder - base) * moves + rank) * units, 0)
                far = jnp.where(near, 0, jnp.clip(offset[source], 0, size))
                here = recv1[chunk][pl.ds(local, units)]
                there = recv2[chunk][pl.ds(far, units)]
                send3[chunk, peer, e] = jnp.where(near, here, there)

        def start3(d, c):
            peer = lax.rem(seat + d, side)
            fill3(peer)
            hop3(chunk, peer, seat).start()
            return c

        lax.fori_loop(1, side, start3, 0)
        fill3(seat)
        own_copy(chunk).start()

    for chunk in range(chunks):

        def finish(d, c):
            peer = lax.rem(seat + d, side)
            sender = lax.rem(seat + side - d, side)
            hop1(chunk, peer, seat).wait_send()
            hop3(chunk, sender, sender).wait_recv()
            hop3(chunk, peer, seat).wait_send()
            return c

        lax.fori_loop(1, side, finish, 0)
        hop2(chunk).wait_send()
        own_copy(chunk).wait()


def arrival_of(anchor, me, slots, moves, slot):
    count = jnp.int32(0)
    for k in range(slots):
        count = count + moved_at(anchor, me * slots + k) * (k <= slot).astype(jnp.int32)
    return jnp.clip(count - 1, 0, moves - 1)


def place_kernel(
    slots, own, anchor, lengths, keys, values, arrived, kept, queries, new_keys, new_values,
    out_k, out_v, out_a
):
    slot = pl.program_id(0)
    index = own[0] * slots + slot
    length = lengths[anchor[index]]
    context, width = keys.shape[1:]
    per_group = queries.shape[1] // (width // HD)
    token_k, token_v = row_of(new_keys, slot), row_of(new_values, slot)

    @pl.when(anchor[index] == index)
    def _():
        out_k[0] = placed(keys[0], token_k, length)
        out_v[0] = placed(values[0], token_v, length)
        out_a[0] = kept[0]

    @pl.when(anchor[index] != index)
    def _():
        def rows_of(kind, head):
            pieces = [
                arrived[kind, head, part, chunk, 0]
                for part in range(arrived.shape[2])
                for chunk in range(arrived.shape[3])
            ]
            return jnp.stack(pieces, axis=1).reshape(context, HD)

        for head in range(width // HD):
            lanes = slice(head * HD, (head + 1) * HD)
            rows = slice(head * per_group, (head + 1) * per_group)
            head_keys = placed(rows_of(0, head), token_k[:, lanes], length)
            head_values = placed(rows_of(1, head), token_v[:, lanes], length)
            out_k[0, :, lanes] = head_keys
            out_v[0, :, lanes] = head_values
            out_a[0, rows] = attend(queries[0, rows], head_keys, head_values, length)


def local(keys, values, lengths, anchor, queries, new_keys, new_values):
    groups = lax.axis_size("dp")
    slots, context, width = keys.shape
    moves = (slots + 1) // 2
    side = groups // 2
    heads_kv = width // HD
    parts = side // (2 * heads_kv)
    chunks = max(1, min(CHUNKS, context // (parts * ROWS)))
    units = context // (parts * chunks * ROWS)
    kind = keys.dtype
    params = functools.partial(pltpu.CompilerParams, vmem_limit_bytes=56 << 20)
    smem = pl.BlockSpec(memory_space=pltpu.SMEM)
    hbm = pl.BlockSpec(memory_space=pl.ANY)

    dma = pltpu.SemaphoreType.DMA
    vmem = pl.BlockSpec(memory_space=pltpu.VMEM)
    heads = queries.shape[1] // HD
    tall = queries.reshape(slots, heads, HD)
    full = side * moves * units
    own = lax.axis_index("dp").reshape(1)
    need, offset, table = pl.pallas_call(
        functools.partial(plan_kernel, groups, slots, moves, units, parts * chunks * ROWS),
        out_shape=(
            jax.ShapeDtypeStruct((1,), jnp.int32),
            jax.ShapeDtypeStruct((groups * slots,), jnp.int32),
            jax.ShapeDtypeStruct((full + units,), jnp.int32),
        ),
        in_specs=[smem, smem, smem],
        out_specs=(smem, smem, smem),
        scratch_shapes=[pltpu.SMEM((groups * slots,), jnp.int32)],
    )(anchor, lengths, own)
    need = lax.pmax(need[0], "parts")
    sizes = sorted({min(full, max(8, int(full * share) // 8 * 8)) for share in SHARES})
    choice = sum((need > size).astype(jnp.int32) for size in sizes[:-1])

    dma = pltpu.SemaphoreType.DMA

    def migrate(number, size):
        return pl.pallas_call(
            functools.partial(migrate_kernel, groups, slots, moves, chunks, size),
            out_shape=(
                jax.ShapeDtypeStruct((side, chunks, moves, units, ROWS, HD), kind),
                jax.ShapeDtypeStruct(tall.shape, tall.dtype),
            ),
            in_specs=[smem, smem, smem, smem, hbm, hbm, vmem, vmem, vmem],
            out_specs=(hbm, vmem),
            scratch_shapes=[
                pltpu.VMEM((2 * slots, units, parts, chunks, ROWS, width), kind),
                pltpu.VMEM((chunks, side, moves * units, ROWS, HD), kind),
                pltpu.VMEM((chunks, size, ROWS, HD), kind),
                pltpu.VMEM((chunks, side, moves, units, ROWS, HD), kind),
            ]
            + [pltpu.VMEM((full, ROWS, HD), kind) for _ in range(chunks)]
            + [pltpu.VMEM((size + units, ROWS, HD), kind) for _ in range(chunks)]
            + [dma((2,)), dma((chunks, side)), dma((chunks, side)), dma((chunks,)), dma((chunks,))]
            + [dma((chunks, side)), dma((chunks, side)), dma((chunks,))],
            compiler_params=params(collective_id=number, has_side_effects=True),
        )

    split = (slots, units, parts, chunks, ROWS, width)
    arrived, kept = lax.switch(
        choice,
        [migrate(number, size) for number, size in enumerate(sizes)],
        anchor,
        lengths,
        offset,
        table,
        keys.reshape(split),
        values.reshape(split),
        tall,
        new_keys,
        new_values,
    )
    arrived = arrived.reshape(2, heads_kv, parts, chunks, moves, units, ROWS, HD)

    def landed(i, own, anchor, lengths):
        return (0, 0, 0, 0, arrival_of(anchor, own[0], slots, moves, i), 0, 0, 0)

    cache = pl.BlockSpec((1, context, width), lambda i, *_: (i, 0, 0))
    token = pl.BlockSpec((slots, width), lambda i, *_: (0, 0))
    query = pl.BlockSpec((1, heads, HD), lambda i, *_: (i, 0, 0))
    cache_keys, cache_values, attended = pl.pallas_call(
        functools.partial(place_kernel, slots),
        out_shape=(
            jax.ShapeDtypeStruct(keys.shape, kind),
            jax.ShapeDtypeStruct(values.shape, kind),
            jax.ShapeDtypeStruct(tall.shape, tall.dtype),
        ),
        grid_spec=pltpu.PrefetchScalarGridSpec(
            num_scalar_prefetch=3,
            grid=(slots,),
            in_specs=[
                cache,
                cache,
                pl.BlockSpec((2, heads_kv, parts, chunks, 1, units, ROWS, HD), landed),
                query,
                query,
                token,
                token,
            ],
            out_specs=(cache, cache, query),
        ),
        compiler_params=params(),
    )(
        own,
        anchor,
        lengths,
        keys,
        values,
        arrived,
        kept,
        tall,
        new_keys,
        new_values,
    )
    return (cache_keys, cache_values, attended.reshape(queries.shape))


def solution(mesh):
    in_specs = (
        P(("parts", "dp"), None, None),
        P(("parts", "dp"), None, None),
        P("parts"),
        P("parts"),
        P(("parts", "dp"), None),
        P(("parts", "dp"), None),
        P(("parts", "dp"), None),
    )
    out_specs = (
        P(("parts", "dp"), None, None),
        P(("parts", "dp"), None, None),
        P(("parts", "dp"), None),
    )
    return jax.shard_map(local, mesh=mesh, in_specs=in_specs, out_specs=out_specs, check_vma=False)
```

```python
import functools
import math

import jax
import jax.numpy as jnp
from jax import lax
from jax.experimental import pallas as pl
from jax.experimental.pallas import tpu as pltpu
from jax.sharding import PartitionSpec as P

HD = 128
ROWS = 16
CHUNKS = 4
SHARES = (0.25, 0.32, 0.38, 0.44, 0.5, 0.58, 1.0)
MESH = pl.DeviceIdType.MESH


def moved_at(anchor, index):
    return (anchor[index] != index).astype(jnp.int32)


def rank_of(anchor, slot, slots):
    first = slot // slots * slots
    count = jnp.int32(0)
    for k in range(slots - 1):
        count = count + moved_at(anchor, first + k) * (first + k < slot).astype(jnp.int32)
    return count


def moved_slot(anchor, group, slots, e):
    found, count = jnp.int32(0), jnp.int32(0)
    for k in range(slots):
        moved = moved_at(anchor, group * slots + k)
        found = found + k * moved * (count == e).astype(jnp.int32)
        count = count + moved
    return found


def row_of(tokens, slot):
    rows = lax.broadcasted_iota(jnp.int32, tokens.shape, 0)
    picked = jnp.where(rows == slot, tokens[...].astype(jnp.float32), 0.0)
    return jnp.sum(picked, axis=0, keepdims=True).astype(tokens.dtype)


def placed(rows, token, length):
    position = lax.broadcasted_iota(jnp.int32, rows.shape, 0)
    tail = jnp.where(position == length, token, jnp.zeros((), rows.dtype))
    return jnp.where(position < length, rows, tail)


def attend(queries, keys, values, length):
    scores = lax.dot_general(
        queries, keys, (((1,), (1,)), ((), ())), preferred_element_type=jnp.float32
    ) / math.sqrt(HD)
    visible = lax.broadcasted_iota(jnp.int32, scores.shape, 1) <= length
    scores = jnp.where(visible, scores, jnp.float32(-1e30))
    powers = jnp.exp(scores - jnp.max(scores, axis=-1, keepdims=True))
    powers = jnp.where(visible, powers, jnp.float32(0.0))
    probs = (powers / jnp.sum(powers, axis=-1, keepdims=True)).astype(jnp.bfloat16)
    result = jnp.dot(probs, values, preferred_element_type=jnp.float32)
    return result.astype(jnp.bfloat16)


def spread_kernel(
    groups, slots, moves, replicas, anchor, lengths, keys, values, queries, new_keys, new_values,
    out, kept, need, offset, table, kv, send1, heard, count_of, following, load_sem, s1_sem,
    r1_sem, own_sem, sn_sem, rn_sem
):
    me, replica = lax.axis_index("dp"), lax.axis_index("parts")
    side = groups // 2
    half, seat = me // side, lax.rem(me, side)
    base = half * side
    units, parts, chunks = kv.shape[1:4]
    width = kv.shape[5]
    heads = width // HD
    context = units * parts * chunks * ROWS

    loads = [
        pltpu.make_async_copy(keys, kv.at[pl.ds(0, slots)], load_sem.at[0]),
        pltpu.make_async_copy(values, kv.at[pl.ds(slots, slots)], load_sem.at[1]),
    ]
    for load in loads:
        load.start()
    barrier = pltpu.get_barrier_semaphore()

    def greet(d, c):
        peer = base + lax.rem(seat + d, side)
        pl.semaphore_signal(barrier, inc=1, device_id={"dp": peer}, device_id_type=MESH)
        return c

    lax.fori_loop(1, side, greet, 0)
    for o in range(1, replicas):
        other = lax.rem(replica + o, replicas)
        pl.semaphore_signal(barrier, inc=1, device_id={"parts": other}, device_id_type=MESH)
    leave = [moved_slot(anchor, me, slots, e) for e in range(moves)]
    for load in loads:
        load.wait()
    pl.semaphore_wait(barrier, side - 1 + replicas - 1)

    def hop1(peer, sender):
        return pltpu.make_async_remote_copy(
            src_ref=send1.at[peer],
            dst_ref=out.at[:, pl.ds(sender * moves * units, moves * units)],
            send_sem=s1_sem.at[peer],
            recv_sem=r1_sem.at[sender],
            device_id={"dp": base + peer},
            device_id_type=MESH,
        )

    def pack(peer):
        column = peer // parts
        lane = pl.multiple_of(lax.rem(column, heads) * HD, HD)
        for e in range(moves):
            for chunk in range(chunks):
                send1[peer, chunk, pl.ds(e * units, units)] = kv[
                    column // heads * slots + leave[e],
                    :,
                    lax.rem(peer, parts),
                    chunk,
                    :,
                    pl.ds(lane, HD),
                ]

    def start1(d, c):
        peer = lax.rem(seat + d, side)
        pack(peer)
        hop1(peer, seat).start()
        return c

    lax.fori_loop(1, side, start1, 0)
    pack(seat)
    own = pltpu.make_async_copy(
        send1.at[seat], out.at[:, pl.ds(seat * moves * units, moves * units)], own_sem
    )
    own.start()

    span = side * slots
    unit_rows = parts * chunks * ROWS
    totals = []
    for to in range(2):

        def count(k, total):
            slot = to * span + k
            source = anchor[slot]
            taken = (lengths[source] + unit_rows - 1) // unit_rows
            taken = jnp.where(source // span != to, taken, 0)
            offset[slot] = total
            count_of[slot] = taken
            return total + taken

        totals.append(lax.fori_loop(0, span, count, jnp.int32(0)))
    need[...] = jnp.full(need.shape, jnp.maximum(totals[0], totals[1]), jnp.int32)

    def tell(o):
        return pltpu.make_async_remote_copy(
            src_ref=need,
            dst_ref=heard.at[o],
            send_sem=sn_sem.at[o],
            recv_sem=rn_sem.at[o],
            device_id={"parts": lax.rem(replica + o, replicas)},
            device_id_type=MESH,
        )

    for o in range(1, replicas):
        tell(o).start()

    target = (1 - half) * span

    def link(k, after):
        slot = target + span - 1 - k
        following[span - 1 - k] = after
        return jnp.where(count_of[slot] > 0, span - 1 - k, after)

    first = lax.fori_loop(0, span, link, jnp.int32(0))

    def walk(u, state):
        k, t = state
        source = anchor[target + k]
        rank = jnp.minimum(rank_of(anchor, source, slots), moves - 1)
        table[u] = (lax.rem(source // slots, side) * moves + rank) * units + t
        done = t + 1 >= count_of[target + k]
        return jnp.where(done, following[k], k), jnp.where(done, 0, t + 1)

    lax.fori_loop(0, table.shape[0], walk, (first, jnp.int32(0)))

    def resident(slot, c):
        length = lengths[me * slots + slot]
        token_k, token_v = row_of(new_keys, slot), row_of(new_values, slot)
        per_group = queries.shape[1] // heads
        for head in range(heads):
            lanes = slice(head * HD, (head + 1) * HD)
            rows = slice(head * per_group, (head + 1) * per_group)
            key_rows = kv[slot, :, :, :, :, lanes].reshape(context, HD)
            value_rows = kv[slots + slot, :, :, :, :, lanes].reshape(context, HD)
            kept[slot, rows] = attend(
                queries[slot, rows],
                placed(key_rows, token_k[:, lanes], length),
                placed(value_rows, token_v[:, lanes], length),
                length,
            )
        return c

    lax.fori_loop(0, slots, resident, 0)

    for o in range(1, replicas):
        tell(o).wait()
    for o in range(1, replicas):
        need[...] = jnp.maximum(need[...], heard[o])

    def finish(d, c):
        peer = lax.rem(seat + d, side)
        sender = lax.rem(seat + side - d, side)
        hop1(sender, sender).wait_recv()
        hop1(peer, seat).wait_send()
        return c

    lax.fori_loop(1, side, finish, 0)
    own.wait()


def deliver_kernel(
    groups, slots, moves, units, size, anchor, offset, table, recv1, out, *scratch
):
    chunks = recv1.shape[0]
    send2, send3 = scratch[:2]
    recv2 = scratch[2 : 2 + chunks]
    s2_sem, r2_sem, s3_sem, r3_sem, own_sem = scratch[2 + chunks :]
    me = lax.axis_index("dp")
    side = groups // 2
    half, seat = me // side, lax.rem(me, side)
    base = half * side
    partner = (1 - half) * side + seat
    barrier = pltpu.get_barrier_semaphore()

    def greet(d, c):
        peer = base + lax.rem(seat + d, side)
        pl.semaphore_signal(barrier, inc=1, device_id={"dp": peer}, device_id_type=MESH)
        return c

    lax.fori_loop(1, side, greet, 0)
    pl.semaphore_signal(barrier, inc=1, device_id={"dp": partner}, device_id_type=MESH)

    def fill2(chunk):
        def step(u, c):
            for k in range(4):
                place = jnp.clip(table[u * 4 + k], 0, recv1.shape[1] - 1)
                send2[chunk, u * 4 + k] = recv1[chunk, place]
            return c

        lax.fori_loop(0, size // 4, step, 0)

    def hop2(chunk):
        return pltpu.make_async_remote_copy(
            src_ref=send2.at[chunk],
            dst_ref=recv2[chunk].at[pl.ds(0, size)],
            send_sem=s2_sem.at[chunk],
            recv_sem=r2_sem.at[chunk],
            device_id={"dp": partner},
            device_id_type=MESH,
        )

    def hop3(chunk, peer, sender):
        return pltpu.make_async_remote_copy(
            src_ref=send3.at[chunk, peer],
            dst_ref=out.at[sender, chunk],
            send_sem=s3_sem.at[chunk, peer],
            recv_sem=r3_sem.at[chunk, sender],
            device_id={"dp": base + peer},
            device_id_type=MESH,
        )

    def own_copy(chunk):
        return pltpu.make_async_copy(send3.at[chunk, seat], out.at[seat, chunk], own_sem.at[chunk])

    fill2(0)
    pl.semaphore_wait(barrier, side)
    for chunk in range(chunks):
        if chunk > 0:
            fill2(chunk)
        hop2(chunk).start()
    for chunk in range(chunks):
        recv2[chunk][pl.ds(size, units)] = jnp.zeros((units, ROWS, HD), recv1.dtype)

    for chunk in range(chunks):
        hop2(chunk).wait_recv()

        def fill3(peer):
            group = base + peer
            for e in range(moves):
                slot = group * slots + moved_slot(anchor, group, slots, e)
                source = anchor[slot]
                rank = jnp.minimum(rank_of(anchor, source, slots), moves - 1)
                holder = source // slots
                near = holder // side == half
                local = jnp.where(near, ((holder - base) * moves + rank) * units, 0)
                far = jnp.where(near, 0, jnp.clip(offset[slot], 0, size))
                here = recv1[chunk, pl.ds(local, units)]
                there = recv2[chunk][pl.ds(far, units)]
                send3[chunk, peer, e] = jnp.where(near, here, there)

        def start3(d, c):
            peer = lax.rem(seat + d, side)
            fill3(peer)
            hop3(chunk, peer, seat).start()
            return c

        lax.fori_loop(1, side, start3, 0)
        fill3(seat)
        own_copy(chunk).start()

    for chunk in range(chunks):

        def finish(d, c):
            peer = lax.rem(seat + d, side)
            sender = lax.rem(seat + side - d, side)
            hop3(chunk, sender, sender).wait_recv()
            hop3(chunk, peer, seat).wait_send()
            return c

        lax.fori_loop(1, side, finish, 0)
        hop2(chunk).wait_send()
        own_copy(chunk).wait()


def arrival_of(anchor, me, slots, moves, slot):
    count = jnp.int32(0)
    for k in range(slots):
        count = count + moved_at(anchor, me * slots + k) * (k <= slot).astype(jnp.int32)
    return jnp.clip(count - 1, 0, moves - 1)


def place_kernel(
    slots, own, anchor, lengths, keys, values, arrived, kept, queries, new_keys, new_values,
    out_k, out_v, out_a
):
    slot = pl.program_id(0)
    index = own[0] * slots + slot
    length = lengths[anchor[index]]
    context, width = keys.shape[1:]
    per_group = queries.shape[1] // (width // HD)
    token_k, token_v = row_of(new_keys, slot), row_of(new_values, slot)

    @pl.when(anchor[index] == index)
    def _():
        out_k[0] = placed(keys[0], token_k, length)
        out_v[0] = placed(values[0], token_v, length)
        out_a[0] = kept[0]

    @pl.when(anchor[index] != index)
    def _():
        def rows_of(kind, head):
            pieces = [
                arrived[kind, head, part, chunk, 0]
                for part in range(arrived.shape[2])
                for chunk in range(arrived.shape[3])
            ]
            return jnp.stack(pieces, axis=1).reshape(context, HD)

        for head in range(width // HD):
            lanes = slice(head * HD, (head + 1) * HD)
            rows = slice(head * per_group, (head + 1) * per_group)
            head_keys = placed(rows_of(0, head), token_k[:, lanes], length)
            head_values = placed(rows_of(1, head), token_v[:, lanes], length)
            out_k[0, :, lanes] = head_keys
            out_v[0, :, lanes] = head_values
            out_a[0, rows] = attend(queries[0, rows], head_keys, head_values, length)


def local(keys, values, lengths, anchor, queries, new_keys, new_values):
    groups = lax.axis_size("dp")
    slots, context, width = keys.shape
    moves = (slots + 1) // 2
    side = groups // 2
    heads_kv = width // HD
    parts = side // (2 * heads_kv)
    chunks = max(1, min(CHUNKS, context // (parts * ROWS)))
    units = context // (parts * chunks * ROWS)
    kind = keys.dtype
    params = functools.partial(pltpu.CompilerParams, vmem_limit_bytes=56 << 20)
    smem = pl.BlockSpec(memory_space=pltpu.SMEM)
    hbm = pl.BlockSpec(memory_space=pl.ANY)

    dma = pltpu.SemaphoreType.DMA
    vmem = pl.BlockSpec(memory_space=pltpu.VMEM)
    heads = queries.shape[1] // HD
    tall = queries.reshape(slots, heads, HD)
    full = side * moves * units
    own = lax.axis_index("dp").reshape(1)
    replicas = lax.axis_size("parts")
    dma = pltpu.SemaphoreType.DMA
    split = (slots, units, parts, chunks, ROWS, width)
    spread, kept, need, offset, table = pl.pallas_call(
        functools.partial(spread_kernel, groups, slots, moves, replicas),
        out_shape=(
            jax.ShapeDtypeStruct((chunks, full, ROWS, HD), kind),
            jax.ShapeDtypeStruct(tall.shape, tall.dtype),
            jax.ShapeDtypeStruct((8, HD), jnp.int32),
            jax.ShapeDtypeStruct((groups * slots,), jnp.int32),
            jax.ShapeDtypeStruct((full,), jnp.int32),
        ),
        in_specs=[smem, smem, hbm, hbm, vmem, vmem, vmem],
        out_specs=(hbm, vmem, vmem, smem, smem),
        scratch_shapes=[
            pltpu.VMEM((2 * slots, units, parts, chunks, ROWS, width), kind),
            pltpu.VMEM((side, chunks, moves * units, ROWS, HD), kind),
            pltpu.VMEM((replicas, 8, HD), jnp.int32),
            pltpu.SMEM((groups * slots,), jnp.int32),
            pltpu.SMEM((side * slots,), jnp.int32),
            dma((2,)),
            dma((side,)),
            dma((side,)),
            dma(()),
            dma((replicas,)),
            dma((replicas,)),
        ],
        compiler_params=params(collective_id=0, has_side_effects=True),
    )(anchor, lengths, keys.reshape(split), values.reshape(split), tall, new_keys, new_values)

    sizes = sorted({min(full, max(8, int(full * share) // 4 * 4)) for share in SHARES})
    choice = sum((need[0, 0] > size).astype(jnp.int32) for size in sizes[:-1])

    def deliver(number, size):
        return pl.pallas_call(
            functools.partial(deliver_kernel, groups, slots, moves, units, size),
            out_shape=jax.ShapeDtypeStruct((side, chunks, moves, units, ROWS, HD), kind),
            in_specs=[smem, smem, smem, vmem],
            out_specs=hbm,
            scratch_shapes=[
                pltpu.VMEM((chunks, size, ROWS, HD), kind),
                pltpu.VMEM((chunks, side, moves, units, ROWS, HD), kind),
            ]
            + [pltpu.VMEM((size + units, ROWS, HD), kind) for _ in range(chunks)]
            + [dma((chunks,)), dma((chunks,))]
            + [dma((chunks, side)), dma((chunks, side)), dma((chunks,))],
            compiler_params=params(collective_id=number + 1, has_side_effects=True),
        )

    arrived = lax.switch(
        choice,
        [deliver(number, size) for number, size in enumerate(sizes)],
        anchor,
        offset,
        table,
        spread,
    )
    arrived = arrived.reshape(2, heads_kv, parts, chunks, moves, units, ROWS, HD)

    def landed(i, own, anchor, lengths):
        return (0, 0, 0, 0, arrival_of(anchor, own[0], slots, moves, i), 0, 0, 0)

    cache = pl.BlockSpec((1, context, width), lambda i, *_: (i, 0, 0))
    token = pl.BlockSpec((slots, width), lambda i, *_: (0, 0))
    query = pl.BlockSpec((1, heads, HD), lambda i, *_: (i, 0, 0))
    cache_keys, cache_values, attended = pl.pallas_call(
        functools.partial(place_kernel, slots),
        out_shape=(
            jax.ShapeDtypeStruct(keys.shape, kind),
            jax.ShapeDtypeStruct(values.shape, kind),
            jax.ShapeDtypeStruct(tall.shape, tall.dtype),
        ),
        grid_spec=pltpu.PrefetchScalarGridSpec(
            num_scalar_prefetch=3,
            grid=(slots,),
            in_specs=[
                cache,
                cache,
                pl.BlockSpec((2, heads_kv, parts, chunks, 1, units, ROWS, HD), landed),
                query,
                query,
                token,
                token,
            ],
            out_specs=(cache, cache, query),
        ),
        compiler_params=params(),
    )(
        own,
        anchor,
        lengths,
        keys,
        values,
        arrived,
        kept,
        tall,
        new_keys,
        new_values,
    )
    return (cache_keys, cache_values, attended.reshape(queries.shape))


def solution(mesh):
    in_specs = (
        P(("parts", "dp"), None, None),
        P(("parts", "dp"), None, None),
        P("parts"),
        P("parts"),
        P(("parts", "dp"), None),
        P(("parts", "dp"), None),
        P(("parts", "dp"), None),
    )
    out_specs = (
        P(("parts", "dp"), None, None),
        P(("parts", "dp"), None, None),
        P(("parts", "dp"), None),
    )
    return jax.shard_map(local, mesh=mesh, in_specs=in_specs, out_specs=out_specs, check_vma=False)
```

```python
import functools
import math

import jax
import jax.numpy as jnp
from jax import lax
from jax.experimental import pallas as pl
from jax.experimental.pallas import tpu as pltpu
from jax.sharding import PartitionSpec as P

HD = 128
ROWS = 16
CHUNKS = 4
SHARES = (0.25, 0.29, 0.32, 0.35, 0.38, 0.41, 0.44, 0.5, 0.58, 1.0)
MESH = pl.DeviceIdType.MESH


def moved_at(anchor, index):
    return (anchor[index] != index).astype(jnp.int32)


def rank_of(anchor, slot, slots):
    first = slot // slots * slots
    count = jnp.int32(0)
    for k in range(slots - 1):
        count = count + moved_at(anchor, first + k) * (first + k < slot).astype(jnp.int32)
    return count


def moved_slot(anchor, group, slots, e):
    found, count = jnp.int32(0), jnp.int32(0)
    for k in range(slots):
        moved = moved_at(anchor, group * slots + k)
        found = found + k * moved * (count == e).astype(jnp.int32)
        count = count + moved
    return found


def row_of(tokens, slot):
    rows = lax.broadcasted_iota(jnp.int32, tokens.shape, 0)
    picked = jnp.where(rows == slot, tokens[...].astype(jnp.float32), 0.0)
    return jnp.sum(picked, axis=0, keepdims=True).astype(tokens.dtype)


def placed(rows, token, length):
    position = lax.broadcasted_iota(jnp.int32, rows.shape, 0)
    tail = jnp.where(position == length, token, jnp.zeros((), rows.dtype))
    return jnp.where(position < length, rows, tail)


def attend(query_row, keys, values, length):
    heads = query_row.shape[1] // HD
    per_group = heads // len(keys)
    query_row = query_row.astype(jnp.float32)
    queries = jnp.concatenate(
        [query_row[:, h * HD : (h + 1) * HD] for h in range(heads)], axis=0
    ).astype(jnp.bfloat16)
    scores = jnp.concatenate(
        [
            lax.dot_general(
                queries[j * per_group : (j + 1) * per_group],
                head_keys,
                (((1,), (1,)), ((), ())),
                preferred_element_type=jnp.float32,
            )
            for j, head_keys in enumerate(keys)
        ],
        axis=0,
    ) / math.sqrt(HD)
    visible = lax.broadcasted_iota(jnp.int32, scores.shape, 1) <= length
    scores = jnp.where(visible, scores, jnp.float32(-1e30))
    powers = jnp.exp(scores - jnp.max(scores, axis=-1, keepdims=True))
    powers = jnp.where(visible, powers, jnp.float32(0.0))
    probs = (powers / jnp.sum(powers, axis=-1, keepdims=True)).astype(jnp.bfloat16)
    results = [
        jnp.dot(
            probs[j * per_group : (j + 1) * per_group],
            head_values,
            preferred_element_type=jnp.float32,
        )
        for j, head_values in enumerate(values)
    ]
    return jnp.concatenate(
        [result[g : g + 1] for result in results for g in range(per_group)], axis=1
    )


def put_row(out, slot, row):
    rows = lax.broadcasted_iota(jnp.int32, out.shape, 0)
    out[...] = jnp.where(rows == slot, row, out[...].astype(jnp.float32)).astype(out.dtype)


def spread_kernel(
    groups, slots, moves, replicas, sizes, anchor, lengths, keys, values, queries, new_keys,
    new_values, out, kept, choice, offset, table, kv, send1, need, heard, count_of, following,
    load_sem, s1_sem, r1_sem, own_sem, sn_sem, rn_sem
):
    me, replica = lax.axis_index("dp"), lax.axis_index("parts")
    side = groups // 2
    half, seat = me // side, lax.rem(me, side)
    base = half * side
    units, parts, chunks = kv.shape[1:4]
    width = kv.shape[5]
    heads = width // HD
    context = units * parts * chunks * ROWS

    loads = [
        pltpu.make_async_copy(keys, kv.at[pl.ds(0, slots)], load_sem.at[0]),
        pltpu.make_async_copy(values, kv.at[pl.ds(slots, slots)], load_sem.at[1]),
    ]
    for load in loads:
        load.start()
    barrier = pltpu.get_barrier_semaphore()

    def greet(d, c):
        peer = base + lax.rem(seat + d, side)
        pl.semaphore_signal(barrier, inc=1, device_id={"dp": peer}, device_id_type=MESH)
        return c

    lax.fori_loop(1, side, greet, 0)
    for o in range(1, replicas):
        other = lax.rem(replica + o, replicas)
        pl.semaphore_signal(barrier, inc=1, device_id={"parts": other}, device_id_type=MESH)
    leave = [moved_slot(anchor, me, slots, e) for e in range(moves)]
    for load in loads:
        load.wait()
    pl.semaphore_wait(barrier, side - 1 + replicas - 1)

    def hop1(peer, sender):
        return pltpu.make_async_remote_copy(
            src_ref=send1.at[peer],
            dst_ref=out.at[:, pl.ds(sender * moves * units, moves * units)],
            send_sem=s1_sem.at[peer],
            recv_sem=r1_sem.at[sender],
            device_id={"dp": base + peer},
            device_id_type=MESH,
        )

    def pack(peer):
        column = peer // parts
        lane = pl.multiple_of(lax.rem(column, heads) * HD, HD)
        for e in range(moves):
            for chunk in range(chunks):
                send1[peer, chunk, pl.ds(e * units, units)] = kv[
                    column // heads * slots + leave[e],
                    :,
                    lax.rem(peer, parts),
                    chunk,
                    :,
                    pl.ds(lane, HD),
                ]

    def start1(d, c):
        peer = lax.rem(seat + d, side)
        pack(peer)
        hop1(peer, seat).start()
        return c

    lax.fori_loop(1, side, start1, 0)
    pack(seat)
    own = pltpu.make_async_copy(
        send1.at[seat], out.at[:, pl.ds(seat * moves * units, moves * units)], own_sem
    )
    own.start()

    span = side * slots
    unit_rows = parts * chunks * ROWS
    totals = []
    for to in range(2):

        def count(k, total):
            slot = to * span + k
            source = anchor[slot]
            taken = (lengths[source] + unit_rows - 1) // unit_rows
            taken = jnp.where(source // span != to, taken, 0)
            offset[slot] = total
            count_of[slot] = taken
            return total + taken

        totals.append(lax.fori_loop(0, span, count, jnp.int32(0)))
    need[...] = jnp.full(need.shape, jnp.maximum(totals[0], totals[1]), jnp.int32)

    def tell(o):
        return pltpu.make_async_remote_copy(
            src_ref=need,
            dst_ref=heard.at[o],
            send_sem=sn_sem.at[o],
            recv_sem=rn_sem.at[o],
            device_id={"parts": lax.rem(replica + o, replicas)},
            device_id_type=MESH,
        )

    for o in range(1, replicas):
        tell(o).start()

    target = (1 - half) * span

    def link(k, after):
        slot = target + span - 1 - k
        following[span - 1 - k] = after
        return jnp.where(count_of[slot] > 0, span - 1 - k, after)

    first = lax.fori_loop(0, span, link, jnp.int32(0))

    def walk(u, state):
        k, t = state
        source = anchor[target + k]
        rank = jnp.minimum(rank_of(anchor, source, slots), moves - 1)
        table[u] = (lax.rem(source // slots, side) * moves + rank) * units + t
        done = t + 1 >= count_of[target + k]
        return jnp.where(done, following[k], k), jnp.where(done, 0, t + 1)

    lax.fori_loop(0, table.shape[0], walk, (first, jnp.int32(0)))

    def resident(slot, c):
        length = lengths[me * slots + slot]
        token_k, token_v = row_of(new_keys, slot), row_of(new_values, slot)
        head_keys, head_values = [], []
        for head in range(heads):
            lanes = slice(head * HD, (head + 1) * HD)
            key_rows = kv[slot, :, :, :, :, lanes].reshape(context, HD)
            value_rows = kv[slots + slot, :, :, :, :, lanes].reshape(context, HD)
            head_keys.append(placed(key_rows, token_k[:, lanes], length))
            head_values.append(placed(value_rows, token_v[:, lanes], length))
        row = attend(row_of(queries, slot), head_keys, head_values, length)
        put_row(kept, slot, row)
        return c

    kept[...] = jnp.zeros(kept.shape, kept.dtype)
    lax.fori_loop(0, slots, resident, 0)

    for o in range(1, replicas):
        tell(o).wait()
    most = need[...]
    for o in range(1, replicas):
        most = jnp.maximum(most, heard[o])
    most = jnp.max(most)
    choice[0] = sum((most > size).astype(jnp.int32) for size in sizes[:-1])

    def finish(d, c):
        peer = lax.rem(seat + d, side)
        sender = lax.rem(seat + side - d, side)
        hop1(sender, sender).wait_recv()
        hop1(peer, seat).wait_send()
        return c

    lax.fori_loop(1, side, finish, 0)
    own.wait()


def deliver_kernel(
    groups, slots, moves, units, size, anchor, offset, table, recv1, out, *scratch
):
    chunks = recv1.shape[0]
    send2, send3 = scratch[:2]
    recv2 = scratch[2 : 2 + chunks]
    s2_sem, r2_sem, s3_sem, r3_sem, own_sem = scratch[2 + chunks :]
    me = lax.axis_index("dp")
    side = groups // 2
    half, seat = me // side, lax.rem(me, side)
    base = half * side
    partner = (1 - half) * side + seat
    barrier = pltpu.get_barrier_semaphore()

    def greet(d, c):
        peer = base + lax.rem(seat + d, side)
        pl.semaphore_signal(barrier, inc=1, device_id={"dp": peer}, device_id_type=MESH)
        return c

    lax.fori_loop(1, side, greet, 0)
    pl.semaphore_signal(barrier, inc=1, device_id={"dp": partner}, device_id_type=MESH)

    def fill2(chunk):
        def step(u, c):
            for k in range(4):
                place = jnp.clip(table[u * 4 + k], 0, recv1.shape[1] - 1)
                send2[chunk, u * 4 + k] = recv1[chunk, place]
            return c

        lax.fori_loop(0, size // 4, step, 0)

    def hop2(chunk):
        return pltpu.make_async_remote_copy(
            src_ref=send2.at[chunk],
            dst_ref=recv2[chunk].at[pl.ds(0, size)],
            send_sem=s2_sem.at[chunk],
            recv_sem=r2_sem.at[chunk],
            device_id={"dp": partner},
            device_id_type=MESH,
        )

    def hop3(chunk, peer, sender):
        return pltpu.make_async_remote_copy(
            src_ref=send3.at[chunk, peer],
            dst_ref=out.at[sender, chunk],
            send_sem=s3_sem.at[chunk, peer],
            recv_sem=r3_sem.at[chunk, sender],
            device_id={"dp": base + peer},
            device_id_type=MESH,
        )

    def own_copy(chunk):
        return pltpu.make_async_copy(send3.at[chunk, seat], out.at[seat, chunk], own_sem.at[chunk])

    fill2(0)
    pl.semaphore_wait(barrier, side)
    for chunk in range(chunks):
        if chunk > 0:
            fill2(chunk)
        hop2(chunk).start()
    for chunk in range(chunks):
        recv2[chunk][pl.ds(size, units)] = jnp.zeros((units, ROWS, HD), recv1.dtype)

    for chunk in range(chunks):
        hop2(chunk).wait_recv()

        def fill3(peer):
            group = base + peer
            for e in range(moves):
                slot = group * slots + moved_slot(anchor, group, slots, e)
                source = anchor[slot]
                rank = jnp.minimum(rank_of(anchor, source, slots), moves - 1)
                holder = source // slots
                near = holder // side == half
                local = jnp.where(near, ((holder - base) * moves + rank) * units, 0)
                far = jnp.where(near, 0, jnp.clip(offset[slot], 0, size))
                here = recv1[chunk, pl.ds(local, units)]
                there = recv2[chunk][pl.ds(far, units)]
                send3[chunk, peer, e] = jnp.where(near, here, there)

        def start3(d, c):
            peer = lax.rem(seat + d, side)
            fill3(peer)
            hop3(chunk, peer, seat).start()
            return c

        lax.fori_loop(1, side, start3, 0)
        fill3(seat)
        own_copy(chunk).start()

    for chunk in range(chunks):

        def finish(d, c):
            peer = lax.rem(seat + d, side)
            sender = lax.rem(seat + side - d, side)
            hop3(chunk, sender, sender).wait_recv()
            hop3(chunk, peer, seat).wait_send()
            return c

        lax.fori_loop(1, side, finish, 0)
        hop2(chunk).wait_send()
        own_copy(chunk).wait()


def arrival_of(anchor, me, slots, moves, slot):
    count = jnp.int32(0)
    for k in range(slots):
        count = count + moved_at(anchor, me * slots + k) * (k <= slot).astype(jnp.int32)
    return jnp.clip(count - 1, 0, moves - 1)


def place_kernel(
    slots, own, anchor, lengths, keys, values, arrived, kept, queries, new_keys, new_values,
    out_k, out_v, out_a
):
    slot = pl.program_id(0)
    index = own[0] * slots + slot
    length = lengths[anchor[index]]
    context, width = keys.shape[1:]
    heads = width // HD
    token_k, token_v = row_of(new_keys, slot), row_of(new_values, slot)

    @pl.when(slot == 0)
    def _():
        out_a[...] = kept[...]

    @pl.when(anchor[index] == index)
    def _():
        for head in range(heads):
            lanes = slice(head * HD, (head + 1) * HD)
            out_k[0, :, lanes] = placed(keys[0, :, lanes], token_k[:, lanes], length)
            out_v[0, :, lanes] = placed(values[0, :, lanes], token_v[:, lanes], length)

    @pl.when(anchor[index] != index)
    def _():
        def rows_of(kind, head):
            pieces = [
                arrived[kind, head, part, chunk, 0]
                for part in range(arrived.shape[2])
                for chunk in range(arrived.shape[3])
            ]
            return jnp.stack(pieces, axis=1).reshape(context, HD)

        head_keys, head_values = [], []
        for head in range(heads):
            lanes = slice(head * HD, (head + 1) * HD)
            head_keys.append(placed(rows_of(0, head), token_k[:, lanes], length))
            head_values.append(placed(rows_of(1, head), token_v[:, lanes], length))
            out_k[0, :, lanes] = head_keys[-1]
            out_v[0, :, lanes] = head_values[-1]
        put_row(out_a, slot, attend(row_of(queries, slot), head_keys, head_values, length))


def local(keys, values, lengths, anchor, queries, new_keys, new_values):
    groups = lax.axis_size("dp")
    slots, context, width = keys.shape
    moves = (slots + 1) // 2
    side = groups // 2
    heads_kv = width // HD
    parts = side // (2 * heads_kv)
    chunks = max(1, min(CHUNKS, context // (parts * ROWS)))
    units = context // (parts * chunks * ROWS)
    kind = keys.dtype
    params = functools.partial(pltpu.CompilerParams, vmem_limit_bytes=56 << 20)
    smem = pl.BlockSpec(memory_space=pltpu.SMEM)
    hbm = pl.BlockSpec(memory_space=pl.ANY)

    dma = pltpu.SemaphoreType.DMA
    vmem = pl.BlockSpec(memory_space=pltpu.VMEM)
    flat = jax.ShapeDtypeStruct(queries.shape, queries.dtype)
    full = side * moves * units
    own = lax.axis_index("dp").reshape(1)
    replicas = lax.axis_size("parts")
    dma = pltpu.SemaphoreType.DMA
    split = (slots, units, parts, chunks, ROWS, width)
    sizes = sorted({min(full, max(8, int(full * share) // 4 * 4)) for share in SHARES})
    spread, kept, choice, offset, table = pl.pallas_call(
        functools.partial(spread_kernel, groups, slots, moves, replicas, sizes),
        out_shape=(
            jax.ShapeDtypeStruct((chunks, full, ROWS, HD), kind),
            flat,
            jax.ShapeDtypeStruct((1,), jnp.int32),
            jax.ShapeDtypeStruct((groups * slots,), jnp.int32),
            jax.ShapeDtypeStruct((full,), jnp.int32),
        ),
        in_specs=[smem, smem, hbm, hbm, vmem, vmem, vmem],
        out_specs=(hbm, vmem, smem, smem, smem),
        scratch_shapes=[
            pltpu.VMEM((2 * slots, units, parts, chunks, ROWS, width), kind),
            pltpu.VMEM((side, chunks, moves * units, ROWS, HD), kind),
            pltpu.VMEM((8, HD), jnp.int32),
            pltpu.VMEM((replicas, 8, HD), jnp.int32),
            pltpu.SMEM((groups * slots,), jnp.int32),
            pltpu.SMEM((side * slots,), jnp.int32),
            dma((2,)),
            dma((side,)),
            dma((side,)),
            dma(()),
            dma((replicas,)),
            dma((replicas,)),
        ],
        compiler_params=params(collective_id=0, has_side_effects=True),
    )(anchor, lengths, keys.reshape(split), values.reshape(split), queries, new_keys, new_values)

    def deliver(number, size):
        return pl.pallas_call(
            functools.partial(deliver_kernel, groups, slots, moves, units, size),
            out_shape=jax.ShapeDtypeStruct((side, chunks, moves, units, ROWS, HD), kind),
            in_specs=[smem, smem, smem, vmem],
            out_specs=hbm,
            scratch_shapes=[
                pltpu.VMEM((chunks, size, ROWS, HD), kind),
                pltpu.VMEM((chunks, side, moves, units, ROWS, HD), kind),
            ]
            + [pltpu.VMEM((size + units, ROWS, HD), kind) for _ in range(chunks)]
            + [dma((chunks,)), dma((chunks,))]
            + [dma((chunks, side)), dma((chunks, side)), dma((chunks,))],
            compiler_params=params(collective_id=number + 1, has_side_effects=True),
        )

    arrived = lax.switch(
        choice[0],
        [deliver(number, size) for number, size in enumerate(sizes)],
        anchor,
        offset,
        table,
        spread,
    )
    arrived = arrived.reshape(2, heads_kv, parts, chunks, moves, units, ROWS, HD)

    def landed(i, own, anchor, lengths):
        return (0, 0, 0, 0, arrival_of(anchor, own[0], slots, moves, i), 0, 0, 0)

    cache = pl.BlockSpec((1, context, width), lambda i, *_: (i, 0, 0))
    token = pl.BlockSpec((slots, width), lambda i, *_: (0, 0))
    query = pl.BlockSpec(queries.shape, lambda i, *_: (0, 0))
    cache_keys, cache_values, attended = pl.pallas_call(
        functools.partial(place_kernel, slots),
        out_shape=(
            jax.ShapeDtypeStruct(keys.shape, kind),
            jax.ShapeDtypeStruct(values.shape, kind),
            flat,
        ),
        grid_spec=pltpu.PrefetchScalarGridSpec(
            num_scalar_prefetch=3,
            grid=(slots,),
            in_specs=[
                cache,
                cache,
                pl.BlockSpec((2, heads_kv, parts, chunks, 1, units, ROWS, HD), landed),
                query,
                query,
                token,
                token,
            ],
            out_specs=(cache, cache, query),
        ),
        compiler_params=params(),
    )(
        own,
        anchor,
        lengths,
        keys,
        values,
        arrived,
        kept,
        queries,
        new_keys,
        new_values,
    )
    return (cache_keys, cache_values, attended)


def solution(mesh):
    in_specs = (
        P(("parts", "dp"), None, None),
        P(("parts", "dp"), None, None),
        P("parts"),
        P("parts"),
        P(("parts", "dp"), None),
        P(("parts", "dp"), None),
        P(("parts", "dp"), None),
    )
    out_specs = (
        P(("parts", "dp"), None, None),
        P(("parts", "dp"), None, None),
        P(("parts", "dp"), None),
    )
    return jax.shard_map(local, mesh=mesh, in_specs=in_specs, out_specs=out_specs, check_vma=False)
```

```python
import functools
import math

import jax
import jax.numpy as jnp
from jax import lax
from jax.experimental import pallas as pl
from jax.experimental.pallas import tpu as pltpu
from jax.sharding import PartitionSpec as P

HD = 128
ROWS = 16
CHUNKS = 4
SHARES = (0.25, 0.29, 0.32, 0.35, 0.38, 0.41, 0.44, 0.5, 0.58, 1.0)
MESH = pl.DeviceIdType.MESH


def moved_at(anchor, index):
    return (anchor[index] != index).astype(jnp.int32)


def rank_of(anchor, slot, slots):
    first = slot // slots * slots
    count = jnp.int32(0)
    for k in range(slots - 1):
        count = count + moved_at(anchor, first + k) * (first + k < slot).astype(jnp.int32)
    return count


def moved_slot(anchor, group, slots, e):
    found, count = jnp.int32(0), jnp.int32(0)
    for k in range(slots):
        moved = moved_at(anchor, group * slots + k)
        found = found + k * moved * (count == e).astype(jnp.int32)
        count = count + moved
    return found


def row_of(tokens, slot):
    rows = lax.broadcasted_iota(jnp.int32, tokens.shape, 0)
    picked = jnp.where(rows == slot, tokens[...].astype(jnp.float32), 0.0)
    return jnp.sum(picked, axis=0, keepdims=True).astype(tokens.dtype)


def placed(rows, token, length):
    position = lax.broadcasted_iota(jnp.int32, rows.shape, 0)
    tail = jnp.where(position == length, token, jnp.zeros((), rows.dtype))
    return jnp.where(position < length, rows, tail)


def attend(query_row, keys, values, length):
    heads = query_row.shape[1] // HD
    per_group = heads // len(keys)
    query_row = query_row.astype(jnp.float32)
    queries = jnp.concatenate(
        [query_row[:, h * HD : (h + 1) * HD] for h in range(heads)], axis=0
    ).astype(jnp.bfloat16)
    scores = jnp.concatenate(
        [
            lax.dot_general(
                queries[j * per_group : (j + 1) * per_group],
                head_keys,
                (((1,), (1,)), ((), ())),
                preferred_element_type=jnp.float32,
            )
            for j, head_keys in enumerate(keys)
        ],
        axis=0,
    ) / math.sqrt(HD)
    visible = lax.broadcasted_iota(jnp.int32, scores.shape, 1) <= length
    scores = jnp.where(visible, scores, jnp.float32(-1e30))
    powers = jnp.exp(scores - jnp.max(scores, axis=-1, keepdims=True))
    powers = jnp.where(visible, powers, jnp.float32(0.0))
    probs = (powers / jnp.sum(powers, axis=-1, keepdims=True)).astype(jnp.bfloat16)
    results = [
        jnp.dot(
            probs[j * per_group : (j + 1) * per_group],
            head_values,
            preferred_element_type=jnp.float32,
        )
        for j, head_values in enumerate(values)
    ]
    return jnp.concatenate(
        [result[g : g + 1] for result in results for g in range(per_group)], axis=1
    )


def put_row(out, slot, row):
    rows = lax.broadcasted_iota(jnp.int32, out.shape, 0)
    out[...] = jnp.where(rows == slot, row, out[...].astype(jnp.float32)).astype(out.dtype)


def spread_kernel(
    groups, slots, moves, replicas, sizes, anchor, lengths, keys, values, queries, new_keys,
    new_values, out, kept, choice, offset, table, kv, send1, need, heard, count_of, following,
    load_sem, s1_sem, r1_sem, own_sem, sn_sem, rn_sem
):
    me, replica = lax.axis_index("dp"), lax.axis_index("parts")
    side = groups // 2
    half, seat = me // side, lax.rem(me, side)
    base = half * side
    units, parts, chunks = kv.shape[1:4]
    width = kv.shape[5]
    heads = width // HD
    context = units * parts * chunks * ROWS

    loads = [
        pltpu.make_async_copy(keys, kv.at[pl.ds(0, slots)], load_sem.at[0]),
        pltpu.make_async_copy(values, kv.at[pl.ds(slots, slots)], load_sem.at[1]),
    ]
    for load in loads:
        load.start()
    barrier = pltpu.get_barrier_semaphore()

    def greet(d, c):
        peer = base + lax.rem(seat + d, side)
        pl.semaphore_signal(barrier, inc=1, device_id={"dp": peer}, device_id_type=MESH)
        return c

    lax.fori_loop(1, side, greet, 0)
    for o in range(1, replicas):
        other = lax.rem(replica + o, replicas)
        pl.semaphore_signal(barrier, inc=1, device_id={"parts": other}, device_id_type=MESH)
    leave = [moved_slot(anchor, me, slots, e) for e in range(moves)]
    for load in loads:
        load.wait()
    pl.semaphore_wait(barrier, side - 1 + replicas - 1)

    def hop1(peer, sender):
        return pltpu.make_async_remote_copy(
            src_ref=send1.at[peer],
            dst_ref=out.at[:, pl.ds(sender * moves * units, moves * units)],
            send_sem=s1_sem.at[peer],
            recv_sem=r1_sem.at[sender],
            device_id={"dp": base + peer},
            device_id_type=MESH,
        )

    def pack(peer):
        column = peer // parts
        lane = pl.multiple_of(lax.rem(column, heads) * HD, HD)
        for e in range(moves):
            for chunk in range(chunks):
                send1[peer, chunk, pl.ds(e * units, units)] = kv[
                    column // heads * slots + leave[e],
                    :,
                    lax.rem(peer, parts),
                    chunk,
                    :,
                    pl.ds(lane, HD),
                ]

    def start1(d, c):
        peer = lax.rem(seat + d, side)
        pack(peer)
        hop1(peer, seat).start()
        return c

    lax.fori_loop(1, side, start1, 0)
    pack(seat)
    own = pltpu.make_async_copy(
        send1.at[seat], out.at[:, pl.ds(seat * moves * units, moves * units)], own_sem
    )
    own.start()

    span = side * slots
    unit_rows = parts * chunks * ROWS
    totals = []
    for to in range(2):

        def count(k, total):
            slot = to * span + k
            source = anchor[slot]
            taken = (lengths[source] + unit_rows - 1) // unit_rows
            taken = jnp.where(source // span != to, taken, 0)
            offset[slot] = total
            count_of[slot] = taken
            return total + taken

        totals.append(lax.fori_loop(0, span, count, jnp.int32(0)))
    need[...] = jnp.full(need.shape, jnp.maximum(totals[0], totals[1]), jnp.int32)

    def tell(o):
        return pltpu.make_async_remote_copy(
            src_ref=need,
            dst_ref=heard.at[o],
            send_sem=sn_sem.at[o],
            recv_sem=rn_sem.at[o],
            device_id={"parts": lax.rem(replica + o, replicas)},
            device_id_type=MESH,
        )

    for o in range(1, replicas):
        tell(o).start()

    target = (1 - half) * span

    def link(k, after):
        slot = target + span - 1 - k
        following[span - 1 - k] = after
        return jnp.where(count_of[slot] > 0, span - 1 - k, after)

    first = lax.fori_loop(0, span, link, jnp.int32(0))

    def walk(u, state):
        k, t = state
        source = anchor[target + k]
        rank = jnp.minimum(rank_of(anchor, source, slots), moves - 1)
        table[u] = (lax.rem(source // slots, side) * moves + rank) * units + t
        done = t + 1 >= count_of[target + k]
        return jnp.where(done, following[k], k), jnp.where(done, 0, t + 1)

    lax.fori_loop(0, table.shape[0], walk, (first, jnp.int32(0)))

    def resident(slot, c):
        length = lengths[me * slots + slot]
        token_k, token_v = row_of(new_keys, slot), row_of(new_values, slot)
        head_keys, head_values = [], []
        for head in range(heads):
            lanes = slice(head * HD, (head + 1) * HD)
            key_rows = kv[slot, :, :, :, :, lanes].reshape(context, HD)
            value_rows = kv[slots + slot, :, :, :, :, lanes].reshape(context, HD)
            head_keys.append(placed(key_rows, token_k[:, lanes], length))
            head_values.append(placed(value_rows, token_v[:, lanes], length))
        row = attend(row_of(queries, slot), head_keys, head_values, length)
        put_row(kept, slot, row)
        return c

    kept[...] = jnp.zeros(kept.shape, kept.dtype)
    lax.fori_loop(0, slots, resident, 0)

    for o in range(1, replicas):
        tell(o).wait()
    most = need[...]
    for o in range(1, replicas):
        most = jnp.maximum(most, heard[o])
    most = jnp.max(most)
    choice[0] = sum((most > size).astype(jnp.int32) for size in sizes[:-1])

    def finish(d, c):
        peer = lax.rem(seat + d, side)
        sender = lax.rem(seat + side - d, side)
        hop1(sender, sender).wait_recv()
        hop1(peer, seat).wait_send()
        return c

    lax.fori_loop(1, side, finish, 0)
    own.wait()


def deliver_kernel(
    groups, slots, moves, units, size, anchor, offset, table, recv1, out, *scratch
):
    chunks = recv1.shape[0]
    send2, send3 = scratch[:2]
    recv2 = scratch[2 : 2 + chunks]
    s2_sem, r2_sem, s3_sem, r3_sem, own_sem = scratch[2 + chunks :]
    me = lax.axis_index("dp")
    side = groups // 2
    half, seat = me // side, lax.rem(me, side)
    base = half * side
    partner = (1 - half) * side + seat
    barrier = pltpu.get_barrier_semaphore()

    def greet(d, c):
        peer = base + lax.rem(seat + d, side)
        pl.semaphore_signal(barrier, inc=1, device_id={"dp": peer}, device_id_type=MESH)
        return c

    lax.fori_loop(1, side, greet, 0)
    pl.semaphore_signal(barrier, inc=1, device_id={"dp": partner}, device_id_type=MESH)

    def fill2(chunk):
        def step(u, c):
            for k in range(4):
                place = jnp.clip(table[u * 4 + k], 0, recv1.shape[1] - 1)
                send2[chunk, u * 4 + k] = recv1[chunk, place]
            return c

        lax.fori_loop(0, size // 4, step, 0)

    def hop2(chunk):
        return pltpu.make_async_remote_copy(
            src_ref=send2.at[chunk],
            dst_ref=recv2[chunk].at[pl.ds(0, size)],
            send_sem=s2_sem.at[chunk],
            recv_sem=r2_sem.at[chunk],
            device_id={"dp": partner},
            device_id_type=MESH,
        )

    def hop3(chunk, peer, sender):
        return pltpu.make_async_remote_copy(
            src_ref=send3.at[chunk, peer],
            dst_ref=out.at[sender, chunk],
            send_sem=s3_sem.at[chunk, peer],
            recv_sem=r3_sem.at[chunk, sender],
            device_id={"dp": base + peer},
            device_id_type=MESH,
        )

    def own_copy(chunk):
        return pltpu.make_async_copy(send3.at[chunk, seat], out.at[seat, chunk], own_sem.at[chunk])

    fill2(0)
    pl.semaphore_wait(barrier, side)
    hop2(0).start()
    for chunk in range(1, chunks):
        fill2(chunk)
    for chunk in range(chunks):
        recv2[chunk][pl.ds(size, units)] = jnp.zeros((units, ROWS, HD), recv1.dtype)

    for chunk in range(chunks):
        hop2(chunk).wait_send()
        if chunk + 1 < chunks:
            hop2(chunk + 1).start()
        hop2(chunk).wait_recv()

        def fill3(peer):
            group = base + peer
            for e in range(moves):
                slot = group * slots + moved_slot(anchor, group, slots, e)
                source = anchor[slot]
                rank = jnp.minimum(rank_of(anchor, source, slots), moves - 1)
                holder = source // slots
                near = holder // side == half
                local = jnp.where(near, ((holder - base) * moves + rank) * units, 0)
                far = jnp.where(near, 0, jnp.clip(offset[slot], 0, size))
                here = recv1[chunk, pl.ds(local, units)]
                there = recv2[chunk][pl.ds(far, units)]
                send3[chunk, peer, e] = jnp.where(near, here, there)

        def start3(d, c):
            peer = lax.rem(seat + d, side)
            fill3(peer)
            hop3(chunk, peer, seat).start()
            return c

        lax.fori_loop(1, side, start3, 0)
        fill3(seat)
        own_copy(chunk).start()

    for chunk in range(chunks):

        def finish(d, c):
            peer = lax.rem(seat + d, side)
            sender = lax.rem(seat + side - d, side)
            hop3(chunk, sender, sender).wait_recv()
            hop3(chunk, peer, seat).wait_send()
            return c

        lax.fori_loop(1, side, finish, 0)
        own_copy(chunk).wait()


def arrival_of(anchor, me, slots, moves, slot):
    count = jnp.int32(0)
    for k in range(slots):
        count = count + moved_at(anchor, me * slots + k) * (k <= slot).astype(jnp.int32)
    return jnp.clip(count - 1, 0, moves - 1)


def place_kernel(
    slots, own, anchor, lengths, keys, values, arrived, kept, queries, new_keys, new_values,
    out_k, out_v, out_a
):
    slot = pl.program_id(0)
    index = own[0] * slots + slot
    length = lengths[anchor[index]]
    context, width = keys.shape[1:]
    heads = width // HD
    token_k, token_v = row_of(new_keys, slot), row_of(new_values, slot)

    @pl.when(slot == 0)
    def _():
        out_a[...] = kept[...]

    @pl.when(anchor[index] == index)
    def _():
        for head in range(heads):
            lanes = slice(head * HD, (head + 1) * HD)
            out_k[0, :, lanes] = placed(keys[0, :, lanes], token_k[:, lanes], length)
            out_v[0, :, lanes] = placed(values[0, :, lanes], token_v[:, lanes], length)

    @pl.when(anchor[index] != index)
    def _():
        def rows_of(kind, head):
            pieces = [
                arrived[kind, head, part, chunk, 0]
                for part in range(arrived.shape[2])
                for chunk in range(arrived.shape[3])
            ]
            return jnp.stack(pieces, axis=1).reshape(context, HD)

        head_keys, head_values = [], []
        for head in range(heads):
            lanes = slice(head * HD, (head + 1) * HD)
            head_keys.append(placed(rows_of(0, head), token_k[:, lanes], length))
            head_values.append(placed(rows_of(1, head), token_v[:, lanes], length))
            out_k[0, :, lanes] = head_keys[-1]
            out_v[0, :, lanes] = head_values[-1]
        put_row(out_a, slot, attend(row_of(queries, slot), head_keys, head_values, length))


def local(keys, values, lengths, anchor, queries, new_keys, new_values):
    groups = lax.axis_size("dp")
    slots, context, width = keys.shape
    moves = (slots + 1) // 2
    side = groups // 2
    heads_kv = width // HD
    parts = side // (2 * heads_kv)
    chunks = max(1, min(CHUNKS, context // (parts * ROWS)))
    units = context // (parts * chunks * ROWS)
    kind = keys.dtype
    params = functools.partial(pltpu.CompilerParams, vmem_limit_bytes=56 << 20)
    smem = pl.BlockSpec(memory_space=pltpu.SMEM)
    hbm = pl.BlockSpec(memory_space=pl.ANY)

    dma = pltpu.SemaphoreType.DMA
    vmem = pl.BlockSpec(memory_space=pltpu.VMEM)
    flat = jax.ShapeDtypeStruct(queries.shape, queries.dtype)
    full = side * moves * units
    own = lax.axis_index("dp").reshape(1)
    replicas = lax.axis_size("parts")
    dma = pltpu.SemaphoreType.DMA
    split = (slots, units, parts, chunks, ROWS, width)
    sizes = sorted({min(full, max(8, int(full * share) // 4 * 4)) for share in SHARES})
    spread, kept, choice, offset, table = pl.pallas_call(
        functools.partial(spread_kernel, groups, slots, moves, replicas, sizes),
        out_shape=(
            jax.ShapeDtypeStruct((chunks, full, ROWS, HD), kind),
            flat,
            jax.ShapeDtypeStruct((1,), jnp.int32),
            jax.ShapeDtypeStruct((groups * slots,), jnp.int32),
            jax.ShapeDtypeStruct((full,), jnp.int32),
        ),
        in_specs=[smem, smem, hbm, hbm, vmem, vmem, vmem],
        out_specs=(hbm, vmem, smem, smem, smem),
        scratch_shapes=[
            pltpu.VMEM((2 * slots, units, parts, chunks, ROWS, width), kind),
            pltpu.VMEM((side, chunks, moves * units, ROWS, HD), kind),
            pltpu.VMEM((8, HD), jnp.int32),
            pltpu.VMEM((replicas, 8, HD), jnp.int32),
            pltpu.SMEM((groups * slots,), jnp.int32),
            pltpu.SMEM((side * slots,), jnp.int32),
            dma((2,)),
            dma((side,)),
            dma((side,)),
            dma(()),
            dma((replicas,)),
            dma((replicas,)),
        ],
        compiler_params=params(collective_id=0, has_side_effects=True),
    )(anchor, lengths, keys.reshape(split), values.reshape(split), queries, new_keys, new_values)

    def deliver(number, size):
        return pl.pallas_call(
            functools.partial(deliver_kernel, groups, slots, moves, units, size),
            out_shape=jax.ShapeDtypeStruct((side, chunks, moves, units, ROWS, HD), kind),
            in_specs=[smem, smem, smem, vmem],
            out_specs=hbm,
            scratch_shapes=[
                pltpu.VMEM((chunks, size, ROWS, HD), kind),
                pltpu.VMEM((chunks, side, moves, units, ROWS, HD), kind),
            ]
            + [pltpu.VMEM((size + units, ROWS, HD), kind) for _ in range(chunks)]
            + [dma((chunks,)), dma((chunks,))]
            + [dma((chunks, side)), dma((chunks, side)), dma((chunks,))],
            compiler_params=params(collective_id=number + 1, has_side_effects=True),
        )

    arrived = lax.switch(
        choice[0],
        [deliver(number, size) for number, size in enumerate(sizes)],
        anchor,
        offset,
        table,
        spread,
    )
    arrived = arrived.reshape(2, heads_kv, parts, chunks, moves, units, ROWS, HD)

    def landed(i, own, anchor, lengths):
        return (0, 0, 0, 0, arrival_of(anchor, own[0], slots, moves, i), 0, 0, 0)

    cache = pl.BlockSpec((1, context, width), lambda i, *_: (i, 0, 0))
    token = pl.BlockSpec((slots, width), lambda i, *_: (0, 0))
    query = pl.BlockSpec(queries.shape, lambda i, *_: (0, 0))
    cache_keys, cache_values, attended = pl.pallas_call(
        functools.partial(place_kernel, slots),
        out_shape=(
            jax.ShapeDtypeStruct(keys.shape, kind),
            jax.ShapeDtypeStruct(values.shape, kind),
            flat,
        ),
        grid_spec=pltpu.PrefetchScalarGridSpec(
            num_scalar_prefetch=3,
            grid=(slots,),
            in_specs=[
                cache,
                cache,
                pl.BlockSpec((2, heads_kv, parts, chunks, 1, units, ROWS, HD), landed),
                query,
                query,
                token,
                token,
            ],
            out_specs=(cache, cache, query),
        ),
        compiler_params=params(),
    )(
        own,
        anchor,
        lengths,
        keys,
        values,
        arrived,
        kept,
        queries,
        new_keys,
        new_values,
    )
    return (cache_keys, cache_values, attended)


def solution(mesh):
    in_specs = (
        P(("parts", "dp"), None, None),
        P(("parts", "dp"), None, None),
        P("parts"),
        P("parts"),
        P(("parts", "dp"), None),
        P(("parts", "dp"), None),
        P(("parts", "dp"), None),
    )
    out_specs = (
        P(("parts", "dp"), None, None),
        P(("parts", "dp"), None, None),
        P(("parts", "dp"), None),
    )
    return jax.shard_map(local, mesh=mesh, in_specs=in_specs, out_specs=out_specs, check_vma=False)
```
